512 devices in a mesh: stn: 32 (over x, z), cell: 16 (over y, core).
Axes of the slice: x: 4, y: 8, z: 8, core: 2. Of those that a mesh axis runs over, the one named last changes fastest.
Arguments:
- sensitivity: bfloat16 [32, 16, 2, 512, 512], P('stn', 'cell'), may hold values from -0.046875 to 0.046875
- block_list: int32 [32, 16, 2], P('stn', 'cell'), may hold values from 0 to 63, as said below
- margin: int32 [1024, 4], P('cell'), may hold values from 0 to 31, as said below
- centres: int32 [16, 1024], P('cell'), may hold values from 0 to 32767
- controls: float32 [16384, 128], P(('stn', 'cell')), may hold values from -4 to 4
- observed: float32 [16384, 128], P(('stn', 'cell')), may hold values from -6 to 6
Outputs:
- updated: float32 [16384, 128], P(('stn', 'cell'))
- residual: float32 [16384, 128], P(('stn', 'cell'))
The draws below stay inside these ranges and needn't reach their ends.
Inputs may be any that keep to these rules, and one draw needn't show every extreme that they name: `block_list`: the 2 cell blocks of one device are distinct. `margin`: the 4 control blocks listed for one cell block are distinct.
All inputs are finite; a program needn't handle non-finite values.
Results may differ from the reference program's by a relative error of at most 0.0003.
Values sent between devices are 32-bit elements; how exact they have to be, the bound alone decides.
A program may use at most 64 MiB of HBM per device.

```python
from functools import partial
import jax
import jax.numpy as jnp
from jax import lax

BLOCK = 512
MEMBERS = 128
SLOTS = 2
CELL_BLOCKS = 64
CENTRES = 32
MARGINS = 4
ITERS = 3
STATIONS = 16384
CONTROL_ROWS = 16384
N_STN = 32
N_CELL = 16


def draw_block_list(key, part):
    key = jax.random.fold_in(key, 11)
    subkeys = jax.random.split(key, N_STN * N_CELL)

    def pick_blocks(subkey):
        return jax.random.permutation(subkey, CELL_BLOCKS)[:SLOTS]
    chosen = jax.vmap(pick_blocks)(subkeys)
    return chosen.reshape(N_STN, N_CELL, SLOTS).astype(jnp.int32)


def draw_margin(key, part):
    key = jax.random.fold_in(key, 23)
    subkeys = jax.random.split(key, N_CELL * CELL_BLOCKS)

    def pick_controls(subkey):
        return jax.random.permutation(subkey, N_STN)[:MARGINS]
    chosen = jax.vmap(pick_controls)(subkeys)
    return chosen.reshape(N_CELL * CELL_BLOCKS, MARGINS).astype(jnp.int32)


def set_ends(values, key, smallest, top_value):
    extent = values.shape
    spot = [jax.random.randint(jax.random.fold_in(key, axis), (), 0, extent[axis]) for axis in range(len(extent))]
    values = values.at[tuple(spot)].set(smallest)
    longest = extent.index(max(extent))
    spot[longest] = (spot[longest] + 1) % extent[longest]
    return values.at[tuple(spot)].set(top_value)


def block_levels(stream_key, shape, cuts, low, high):
    def one(dim, shards_of):
        heights = jax.random.uniform(jax.random.fold_in(jax.random.fold_in(stream_key, 6), dim), (shards_of,), jnp.float32, low / len(cuts), high / len(cuts))
        return jnp.repeat(jnp.exp(heights), shape[dim] // shards_of).reshape((-1,) + (1,) * (len(shape) - dim - 1))

    factor_of = one(*cuts[0])
    for cut in cuts[1:]:
        factor_of = factor_of * one(*cut)
    return factor_of


def normal_values(key, extent, scale, bound, cuts=(), held_as=jnp.bfloat16):
    drawn = scale * jax.random.normal(key, extent, jnp.float32)
    if cuts:
        drawn = drawn * block_levels(key, extent, cuts, -0.22, 0.18)
    return jnp.clip(drawn, -bound, bound).astype(held_as)


def setup_inputs(seed: int = 0) -> dict:
    key_list = jax.random.split(jax.random.key(seed), 7)
    sensitivity = normal_values(key_list[0], (N_STN, N_CELL, SLOTS, BLOCK, BLOCK), (N_CELL * SLOTS * BLOCK) ** -0.5, 0.046875, ((0, 32), (1, 16)))
    block_list = draw_block_list(jax.random.fold_in(key_list[6], 71), 0)
    margin = draw_margin(jax.random.fold_in(key_list[6], 71), 0)
    centres = set_ends(jax.random.randint(key_list[3], (N_CELL, N_STN * CENTRES), 0, CELL_BLOCKS * BLOCK), jax.random.fold_in(key_list[3], 1), 0, (CELL_BLOCKS * BLOCK) - 1).astype(jnp.int32)
    controls = normal_values(key_list[4], (CONTROL_ROWS, MEMBERS), 0.6, 4.0, ((0, 512),), jnp.float32)
    observed = normal_values(key_list[5], (STATIONS, MEMBERS), 1.0, 6.0, ((0, 512),), jnp.float32)
    return dict(sensitivity=sensitivity, block_list=block_list, margin=margin, centres=centres, controls=controls, observed=observed)


rbf_radius = 10.0


def gaussian(cell_ids, centre_ids):
    squared = jnp.zeros(cell_ids.shape + (centre_ids.shape[-1],), jnp.float32)
    for divisor, modulus in ((1024, 1073741824), (32, 32), (1, 32)):
        cell_coord = ((cell_ids // divisor) % modulus).astype(jnp.float32)
        centre_coord = ((centre_ids // divisor) % modulus).astype(jnp.float32)
        spread = cell_coord[..., :, None] - centre_coord[..., None, :]
        squared = squared + spread * spread
    return jnp.exp(squared * (-0.5 / (rbf_radius * rbf_radius)))


def slot_basis(blocks, margin_rows, centre_row, block_size, centre_count):
    offsets = jnp.arange(block_size, dtype=jnp.int32)
    cell_ids = blocks[:, None].astype(jnp.int32) * block_size + offsets[None, :]
    listed = margin_rows[blocks]
    within = jnp.arange(centre_count, dtype=jnp.int32)
    slot_ids = listed[:, :, None].astype(jnp.int32) * centre_count + within[None, None, :]
    centre_ids = centre_row[slot_ids.reshape(blocks.shape[0], -1)]
    return gaussian(cell_ids, centre_ids)


def station_of(sens_group, values):
    return jnp.einsum('cnij,cnjk->ik', sens_group.astype(jnp.float32), values, precision=lax.Precision.HIGHEST)


def reference(sensitivity, block_list, margin, centres, controls, observed):
    stn_count = N_STN
    cell_count = N_CELL
    members = MEMBERS
    margin_grid = margin.reshape(cell_count, CELL_BLOCKS, MARGINS)
    column = jnp.arange(cell_count, dtype=jnp.int32)
    listed = margin_grid[column[None, :, None], block_list]
    basis_maker = jax.vmap(partial(slot_basis, block_size=BLOCK, centre_count=CENTRES))

    def phi_for(vector, blocks_row, listed_group):
        layout = vector.reshape(stn_count, cell_count, CENTRES, members)
        picked = layout[listed_group, column[:, None, None]]
        picked = picked.reshape(cell_count, SLOTS, MARGINS * CENTRES, members)
        basis_group = basis_maker(blocks_row, margin_grid, centres)
        return jnp.einsum('cnib,cnbk->cnik', basis_group, picked, precision=lax.Precision.HIGHEST)

    def start_group(pieces):
        sens_group, blocks_row, listed_group = pieces
        tanh_phi = jnp.tanh(phi_for(controls, blocks_row, listed_group))
        density = 0.5 * (1.0 + tanh_phi)
        slope_group = 0.5 * (1.0 - tanh_phi * tanh_phi)
        return slope_group, station_of(sens_group, density)

    slopes, predicted = lax.map(start_group, (sensitivity, block_list, listed))

    def image_of(vector):
        def one_group(pieces):
            sens_group, blocks_row, listed_group, slope_group = pieces
            phi = phi_for(vector, blocks_row, listed_group)
            return station_of(sens_group, slope_group * phi)
        return lax.map(one_group, (sensitivity, block_list, listed, slopes)).reshape(-1, members)

    def adjoint(residual):
        rows_all = residual.reshape(stn_count, BLOCK, members)

        def one_group(carry, pieces):
            sens_group, blocks_row, listed_group, slope_group, rows_group = pieces
            pulled = jnp.einsum('cnij,ik->cnjk', sens_group.astype(jnp.float32), rows_group, precision=lax.Precision.HIGHEST)
            weighted = slope_group * pulled
            basis_group = basis_maker(blocks_row, margin_grid, centres)
            contribution = jnp.einsum('cnib,cnik->cnbk', basis_group, weighted, precision=lax.Precision.HIGHEST)
            contribution = contribution.reshape(cell_count, SLOTS, MARGINS, CENTRES, members)
            onehot = (listed_group[..., None] == jnp.arange(stn_count, dtype=jnp.int32)).astype(jnp.float32)
            group_part = jnp.einsum('cnoj,cnobk->cjbk', onehot, contribution, precision=lax.Precision.HIGHEST)
            return carry + group_part, None

        start = jnp.zeros((cell_count, stn_count, CENTRES, members), jnp.float32)
        summed, unused = lax.scan(one_group, start, (sensitivity, block_list, listed, slopes, rows_all))
        return jnp.transpose(summed, (1, 0, 2, 3)).reshape(-1, members)

    residual = observed - predicted.reshape(-1, members)
    gradient = adjoint(residual)
    grad_norm = jnp.sum(gradient * gradient, 0)
    direction = gradient
    update = jnp.zeros_like(controls)
    for iteration in range(ITERS):
        image_vec = image_of(direction)
        curvature = jnp.sum(image_vec * image_vec, 0)
        step_size = grad_norm / curvature
        update = update + step_size * direction
        residual = residual - step_size * image_vec
        if iteration + 1 < ITERS:
            gradient = adjoint(residual)
            new_norm = jnp.sum(gradient * gradient, 0)
            direction = gradient + (new_norm / grad_norm) * direction
            grad_norm = new_norm
    return controls + update, residual
```

```python
import jax
import jax.numpy as jnp
from jax import lax
from jax.experimental import pallas as pl
from jax.experimental.pallas import tpu as pltpu
from jax.sharding import PartitionSpec as P

MESH = pl.DeviceIdType.MESH
ITERS = 3
SLOTS, BLOCK, MARGINS, CENTRES, MEMBERS = 2, 512, 4, 32, 128
NX, NZ, NY = 4, 8, 8
NSTN, NCELL = NX * NZ, NY * 2
F32, BF16 = jnp.float32, jnp.bfloat16


def split(value):
    high = value.astype(BF16)
    low = (value - high.astype(F32)).astype(BF16)
    return high, low


def column_sum(value):
    return jnp.sum(value.reshape(-1, MEMBERS), axis=0, keepdims=True)


def kernel(
    sens_hbm, blocks, margin, centres, controls, observed, updated, final_residual,
    sens, sens_t, basis, basis_t, coeff_rhs, cell_rhs, row_rhs, slope,
    gath, part, core_in, paired, y_in, full, grouped, x_in, x_sum, z_in,
    own_grad, own_dir, own_image, own_res, own_upd,
    row_core, row_core_in, row_y, row_y_in, row_x, row_x_in, row_z, row_z_in,
    sens_sem, gz_s, gz_r, gx_s, gx_r, c_s, c_r, y_s, y_r, fy_s, fy_r, fc_s, fc_r, dx_s, dx_r, dz_s, dz_r,
    rc_s, rc_r, ry_s, ry_r, rx_s, rx_r, rz_s, rz_r,
):
    stn, cell = lax.axis_index("stn"), lax.axis_index("cell")
    x, z = stn // NZ, stn % NZ
    y, core = cell // 2, cell % 2
    x_peers = [((x + d) % NX, ((x + d) % NX) * NZ + z, cell) for d in range(1, NX)]
    z_peers = [((z + d) % NZ, x * NZ + (z + d) % NZ, cell) for d in range(1, NZ)]
    y_peers = [((y + d) % NY, stn, ((y + d) % NY) * 2 + core) for d in range(1, NY)]
    core_peer = (1 - core, stn, y * 2 + 1 - core)

    def send(src, dst, ssem, rsem, peer):
        pltpu.make_async_remote_copy(
            src_ref=src, dst_ref=dst, send_sem=ssem, recv_sem=rsem,
            device_id={"stn": peer[1], "cell": peer[2]}, device_id_type=MESH,
        ).start()

    def drain(ref, sem):
        pltpu.make_async_copy(ref, ref, sem).wait()

    barrier = pltpu.get_barrier_semaphore()
    everyone = x_peers + z_peers + y_peers + [core_peer]
    for peer in everyone:
        pl.semaphore_signal(
            barrier, inc=1, device_id={"stn": peer[1], "cell": peer[2]}, device_id_type=MESH
        )
    load = pltpu.make_async_copy(sens_hbm, sens, sens_sem)
    load.start()
    gath[0, stn] = controls[...]
    pl.semaphore_wait(barrier, len(everyone))

    def gather_z(k):
        for peer in z_peers:
            send(gath.at[k, stn], gath.at[k, stn], gz_s.at[k], gz_r.at[k], peer)

    def gather_x(k):
        drain(gath.at[k, 0:NZ - 1], gz_r.at[k])
        rows = pl.ds(x * NZ, NZ)
        for peer in x_peers:
            send(gath.at[k, rows], gath.at[k, rows], gx_s.at[k], gx_r.at[k], peer)

    def gather_end(k):
        drain(gath.at[k, 0:NSTN - NZ], gx_r.at[k])

    gather_z(0)

    lane = lax.broadcasted_iota(jnp.int32, (8, MEMBERS), 1)
    rows_of_centres = [
        jnp.broadcast_to(centres[0:1, i * MEMBERS:(i + 1) * MEMBERS], (8, MEMBERS)) for i in range(8)
    ]
    listed = []
    for n in range(SLOTS):
        block = blocks[n]
        listed.append([margin[block, o] for o in range(MARGINS)])
        centre = jnp.zeros((8, MEMBERS), jnp.int32)
        for o in range(MARGINS):
            j = listed[n][o]
            row = rows_of_centres[0]
            for i in range(1, 8):
                row = jnp.where(j // 4 == i, rows_of_centres[i], row)
            turned = row
            for i in range(1, 4):
                turned = jnp.where((o + 4 - j % 4) % 4 == i, pltpu.roll(row, i * CENTRES, 1), turned)
            centre = jnp.where(lane // CENTRES == o, turned, centre)
        centre = centre[0:1]
        cells = lax.broadcasted_iota(jnp.int32, (BLOCK, MEMBERS), 0) + block * BLOCK
        squared = jnp.zeros((BLOCK, MEMBERS), F32)
        for shift, mask in ((10, 1048575), (5, 31), (0, 31)):
            cell_coord = ((cells >> shift) & mask).astype(F32)
            centre_coord = ((centre >> shift) & mask).astype(F32)
            spread = cell_coord - centre_coord
            squared = squared + spread * spread
        table = jnp.exp(squared * (-0.5 / 100.0))
        high, low = split(table)
        basis[n, :, 0:MEMBERS] = high
        basis[n, :, MEMBERS:] = low
        high, low = split(table.T)
        basis_t[n, 0:MEMBERS] = high
        basis_t[n, MEMBERS:] = low

    gather_x(0)
    load.wait()
    for n in range(SLOTS):
        for i in range(4):
            piece = sens[n, i * 128:(i + 1) * 128, :]
            sens_t[n, :, i * 128:(i + 1) * 128] = piece.T
    gather_end(0)

    def field(k, n):
        for o in range(MARGINS):
            high, low = split(gath[k, listed[n][o]])
            for base in (0, MEMBERS):
                at = slice(base + o * CENTRES, base + (o + 1) * CENTRES)
                coeff_rhs[n, at, 0:MEMBERS] = high
                coeff_rhs[n, at, MEMBERS:] = low
        both = jnp.dot(basis[n], coeff_rhs[n], preferred_element_type=F32)
        return both[:, 0:MEMBERS] + both[:, MEMBERS:]

    def station(k):
        both = jnp.dot(sens[0], cell_rhs[0], preferred_element_type=F32)
        both += jnp.dot(sens[1], cell_rhs[1], preferred_element_type=F32)
        part[k] = (both[:, 0:MEMBERS] + both[:, MEMBERS:]).reshape(NCELL // 2, 2, CENTRES, MEMBERS)

    def put_cells(n, value):
        high, low = split(value)
        cell_rhs[n, :, 0:MEMBERS] = high
        cell_rhs[n, :, MEMBERS:] = low

    def sum_cells(k, with_norm):
        send(part.at[k, :, 1 - core], core_in.at[k], c_s.at[k], c_r.at[k], core_peer)
        drain(core_in.at[k], c_r.at[k])
        paired[k] = part[k, :, core] + core_in[k]
        for peer in y_peers:
            send(paired.at[k, peer[0]], y_in.at[k, y], y_s.at[k], y_r.at[k], peer)
        y_in[k, y] = paired[k, y]
        norm = None
        if with_norm:
            drain(row_core_in.at[k], rc_r.at[k])
            row_y[k] = row_core[k] + row_core_in[k]
            for peer in y_peers:
                send(row_y.at[k], row_y_in.at[k, y], ry_s.at[k], ry_r.at[k], peer)
            row_y_in[k, y] = row_y[k]
            drain(row_y_in.at[k, 0:NY - 1], ry_r.at[k])
            norm = sum(row_y_in[k, i] for i in range(NY))
        drain(y_in.at[k, 0:NY - 1], y_r.at[k])
        return sum(y_in[k, i] for i in range(NY)), norm

    def gather_cells(k, rows):
        full[k, y, core] = rows
        for peer in y_peers:
            send(full.at[k, y, core], full.at[k, y, core], fy_s.at[k], fy_r.at[k], peer)
        drain(full.at[k, 0:NY - 1, 0], fy_r.at[k])
        send(full.at[k, :, core], full.at[k, :, core], fc_s.at[k], fc_r.at[k], core_peer)
        drain(full.at[k, :, 0], fc_r.at[k])

    def adjoint(k, with_curvature):
        rows = full[k].reshape(BLOCK, MEMBERS)
        if with_curvature:
            row_x[k] = column_sum(rows * rows)
            for peer in x_peers:
                send(row_x.at[k], row_x_in.at[k, x], rx_s.at[k], rx_r.at[k], peer)
            row_x_in[k, x] = row_x[k]
        high, low = split(rows)
        row_rhs[:, 0:MEMBERS] = high
        row_rhs[:, MEMBERS:] = low
        parts = []
        for n in range(SLOTS):
            pulled = jnp.dot(sens_t[n], row_rhs[...], preferred_element_type=F32)
            put_cells(n, slope[n] * (pulled[:, 0:MEMBERS] + pulled[:, MEMBERS:]))
            four = jnp.dot(basis_t[n], cell_rhs[n], preferred_element_type=F32)
            two = four[:, 0:MEMBERS] + four[:, MEMBERS:]
            parts.append((two[0:MEMBERS] + two[MEMBERS:]).reshape(MARGINS, CENTRES, MEMBERS))
        for j in range(NSTN):
            total = None
            for n in range(SLOTS):
                for o in range(MARGINS):
                    term = jnp.where(listed[n][o] == j, parts[n][o], 0.0)
                    total = term if total is None else total + term
            grouped[k, j // NZ, j % NZ] = total
        for peer in x_peers:
            send(grouped.at[k, peer[0]], x_in.at[k, x], dx_s.at[k], dx_r.at[k], peer)
        x_in[k, x] = grouped[k, x]
        drain(x_in.at[k, 0:NX - 1], dx_r.at[k])
        x_sum[k] = sum(x_in[k, i] for i in range(NX))
        for peer in z_peers:
            send(x_sum.at[k, peer[0]], z_in.at[k, z], dz_s.at[k], dz_r.at[k], peer)
        z_in[k, z] = x_sum[k, z]
        curvature = None
        if with_curvature:
            drain(row_x_in.at[k, 0:NX - 1], rx_r.at[k])
            row_z[k] = sum(row_x_in[k, i] for i in range(NX))
            for peer in z_peers:
                send(row_z.at[k], row_z_in.at[k, z], rz_s.at[k], rz_r.at[k], peer)
            row_z_in[k, z] = row_z[k]
            drain(row_z_in.at[k, 0:NZ - 1], rz_r.at[k])
            curvature = sum(row_z_in[k, i] for i in range(NZ))
        drain(z_in.at[k, 0:NZ - 1], dz_r.at[k])
        return sum(z_in[k, i] for i in range(NZ)), curvature

    for n in range(SLOTS):
        tanh_phi = jnp.tanh(field(0, n))
        slope[n] = 0.5 * (1.0 - tanh_phi * tanh_phi)
        put_cells(n, 0.5 * (1.0 + tanh_phi))
    station(0)
    predicted, _ = sum_cells(0, False)
    own_res[...] = observed[...] - predicted
    gather_cells(0, own_res[...])
    gradient, _ = adjoint(0, False)
    own_grad[...] = gradient

    norm = None
    for k in range(1, ITERS + 1):
        gath[k, stn] = own_grad[...]
        gather_z(k)
        gather_x(k)
        gather_end(k)
        row_core[k] = column_sum(gath[k] * gath[k])
        send(row_core.at[k], row_core_in.at[k], rc_s.at[k], rc_r.at[k], core_peer)
        for n in range(SLOTS):
            put_cells(n, slope[n] * field(k, n))
        station(k)
        image, new_norm = sum_cells(k, True)
        direction = own_grad[...]
        if k > 1:
            ratio = new_norm / norm
            image = image + ratio * own_image[...]
            direction = direction + ratio * own_dir[...]
        norm = new_norm
        own_image[...] = image
        own_dir[...] = direction
        if k < ITERS:
            gather_cells(k, image)
            change, curvature = adjoint(k, True)
            step = norm / curvature
            own_grad[...] = own_grad[...] - step * change
        else:
            row_core[0] = column_sum(image * image)
            send(row_core.at[0], row_core_in.at[0], rc_s.at[0], rc_r.at[0], core_peer)
            drain(row_core_in.at[0], rc_r.at[0])
            row_y[0] = row_core[0] + row_core_in[0]
            for peer in y_peers:
                send(row_y.at[0], row_y_in.at[0, y], ry_s.at[0], ry_r.at[0], peer)
            row_y_in[0, y] = row_y[0]
            drain(row_y_in.at[0, 0:NY - 1], ry_r.at[0])
            row_x[0] = sum(row_y_in[0, i] for i in range(NY))
            for peer in x_peers:
                send(row_x.at[0], row_x_in.at[0, x], rx_s.at[0], rx_r.at[0], peer)
            row_x_in[0, x] = row_x[0]
            drain(row_x_in.at[0, 0:NX - 1], rx_r.at[0])
            row_z[0] = sum(row_x_in[0, i] for i in range(NX))
            for peer in z_peers:
                send(row_z.at[0], row_z_in.at[0, z], rz_s.at[0], rz_r.at[0], peer)
            row_z_in[0, z] = row_z[0]
            drain(row_z_in.at[0, 0:NZ - 1], rz_r.at[0])
            step = norm / sum(row_z_in[0, i] for i in range(NZ))
        own_res[...] = own_res[...] - step * image
        own_upd[...] = step * direction if k == 1 else own_upd[...] + step * direction

    updated[...] = controls[...] + own_upd[...]
    final_residual[...] = own_res[...]

    for k in range(ITERS + 1):
        drain(gath.at[k, 0:NZ - 1], gz_s.at[k])
        drain(gath.at[k, 0:NSTN - NZ], gx_s.at[k])
        drain(core_in.at[k], c_s.at[k])
        drain(y_in.at[k, 0:NY - 1], y_s.at[k])
        drain(row_core_in.at[k], rc_s.at[k])
        drain(row_y_in.at[k, 0:NY - 1], ry_s.at[k])
    for k in range(ITERS):
        drain(full.at[k, 0:NY - 1, 0], fy_s.at[k])
        drain(full.at[k, :, 0], fc_s.at[k])
        drain(x_in.at[k, 0:NX - 1], dx_s.at[k])
        drain(z_in.at[k, 0:NZ - 1], dz_s.at[k])
        drain(row_x_in.at[k, 0:NX - 1], rx_s.at[k])
        drain(row_z_in.at[k, 0:NZ - 1], rz_s.at[k])


def local(sensitivity, block_list, margin, centres, controls, observed):
    rows = (CENTRES, MEMBERS)
    a, d = ITERS + 1, ITERS

    def vmem(*shape):
        return pltpu.VMEM(shape, F32)

    scratch = [
        pltpu.VMEM((SLOTS, BLOCK, BLOCK), BF16),
        pltpu.VMEM((SLOTS, BLOCK, BLOCK), BF16),
        pltpu.VMEM((SLOTS, BLOCK, 2 * MEMBERS), BF16),
        pltpu.VMEM((SLOTS, 2 * MEMBERS, BLOCK), BF16),
        pltpu.VMEM((SLOTS, 2 * MEMBERS, 2 * MEMBERS), BF16),
        pltpu.VMEM((SLOTS, BLOCK, 2 * MEMBERS), BF16),
        pltpu.VMEM((BLOCK, 2 * MEMBERS), BF16),
        vmem(SLOTS, BLOCK, MEMBERS),
        vmem(a, NSTN, *rows),
        vmem(a, NY, 2, *rows),
        vmem(a, NY, *rows),
        vmem(a, NY, *rows),
        vmem(a, NY, *rows),
        vmem(d, NY, 2, *rows),
        vmem(d, NX, NZ, *rows),
        vmem(d, NX, NZ, *rows),
        vmem(d, NZ, *rows),
        vmem(d, NZ, *rows),
        vmem(*rows), vmem(*rows), vmem(*rows), vmem(*rows), vmem(*rows),
        vmem(a, 1, MEMBERS), vmem(a, 1, MEMBERS),
        vmem(a, 1, MEMBERS), vmem(a, NY, 1, MEMBERS),
        vmem(d, 1, MEMBERS), vmem(d, NX, 1, MEMBERS),
        vmem(d, 1, MEMBERS), vmem(d, NZ, 1, MEMBERS),
        pltpu.SemaphoreType.DMA,
    ]
    scratch += [pltpu.SemaphoreType.DMA((a,))] * 8
    scratch += [pltpu.SemaphoreType.DMA((d,))] * 8
    scratch += [pltpu.SemaphoreType.DMA((a,))] * 4
    scratch += [pltpu.SemaphoreType.DMA((d,))] * 4
    in_vmem = pl.BlockSpec(memory_space=pltpu.VMEM)
    in_smem = pl.BlockSpec(memory_space=pltpu.SMEM)
    return pl.pallas_call(
        kernel,
        out_shape=(jax.ShapeDtypeStruct(rows, F32), jax.ShapeDtypeStruct(rows, F32)),
        in_specs=[pl.BlockSpec(memory_space=pl.ANY), in_smem, in_smem, in_vmem, in_vmem, in_vmem],
        out_specs=(in_vmem, in_vmem),
        scratch_shapes=scratch,
        compiler_params=pltpu.CompilerParams(
            collective_id=0, has_side_effects=True, vmem_limit_bytes=40 * 1024 * 1024
        ),
        cost_estimate=pl.CostEstimate(flops=3_000_000_000, bytes_accessed=2_000_000, transcendentals=262144),
        name="gauss_newton",
    )(
        sensitivity.reshape(SLOTS, BLOCK, BLOCK), block_list.reshape(SLOTS), margin, centres,
        controls, observed,
    )


def solution(mesh):
    return jax.shard_map(
        local,
        mesh=mesh,
        in_specs=(
            P("stn", "cell", None, None, None),
            P("stn", "cell", None),
            P("cell", None),
            P("cell", None),
            P(("stn", "cell"), None),
            P(("stn", "cell"), None),
        ),
        out_specs=(P(("stn", "cell"), None), P(("stn", "cell"), None)),
        check_vma=False,
    )
```

```python
import jax
import jax.numpy as jnp
from jax import lax
from jax.experimental import pallas as pl
from jax.experimental.pallas import tpu as pltpu
from jax.sharding import PartitionSpec as P

MESH = pl.DeviceIdType.MESH
ITERS = 3
SLOTS, BLOCK, MARGINS, CENTRES, MEMBERS = 2, 512, 4, 32, 128
NX, NZ, NY = 4, 8, 8
NSTN, NCELL = NX * NZ, NY * 2
F32, BF16 = jnp.float32, jnp.bfloat16


def split(value):
    high = value.astype(BF16)
    low = (value - high.astype(F32)).astype(BF16)
    return high, low


def column_sum(value):
    return jnp.sum(value.reshape(-1, MEMBERS), axis=0, keepdims=True)


def interleave(first, second):
    upper = lax.broadcasted_iota(jnp.int32, first.shape, 1) < MARGINS
    even = jnp.where(upper, first, pltpu.roll(second, MARGINS, 1))
    odd = jnp.where(upper, pltpu.roll(first, MARGINS, 1), second)
    return even, odd


def kernel(
    sens_hbm, blocks, margin, centres, controls, observed, updated, final_residual,
    sens, sens_t, basis, basis_r, basis_t, coeff_rhs, cell_rhs, row_rhs, slope,
    list_in, hot, hot_t, grad_rhs, entry_rhs,
    gath, part, core_in, paired, y_in, full, scat_out, scat_in, ans_out, ans_in,
    own_grad, own_dir, own_image, own_res, own_upd,
    row_core, row_core_in, row_y, row_y_in, row_s, row_s_in, pair_out, pair_in,
    sens_sem, li_s, li_r, gz_s, gz_r, gx_s, gx_r, c_s, c_r, y_s, y_r, fy_s, fy_r, fc_s, fc_r,
    sc_s, sc_r, an_s, an_r, rc_s, rc_r, ry_s, ry_r, rs_s, rs_r, pr_s, pr_r,
):
    stn, cell = lax.axis_index("stn"), lax.axis_index("cell")
    x, z = stn // NZ, stn % NZ
    y, core = cell // 2, cell % 2
    x_peers = [((x + d) % NX, ((x + d) % NX) * NZ + z, cell) for d in range(1, NX)]
    z_peers = [((z + d) % NZ, x * NZ + (z + d) % NZ, cell) for d in range(1, NZ)]
    y_peers = [((y + d) % NY, stn, ((y + d) % NY) * 2 + core) for d in range(1, NY)]
    core_peer = (1 - core, stn, y * 2 + 1 - core)
    s_peers = [((stn + d) % NSTN, (stn + d) % NSTN, cell) for d in range(1, NSTN)]

    def send(src, dst, ssem, rsem, peer):
        pltpu.make_async_remote_copy(
            src_ref=src, dst_ref=dst, send_sem=ssem, recv_sem=rsem,
            device_id={"stn": peer[1], "cell": peer[2]}, device_id_type=MESH,
        ).start()

    def drain(ref, sem):
        pltpu.make_async_copy(ref, ref, sem).wait()

    barrier = pltpu.get_barrier_semaphore()
    everyone = s_peers + y_peers + [core_peer]
    for peer in everyone:
        pl.semaphore_signal(
            barrier, inc=1, device_id={"stn": peer[1], "cell": peer[2]}, device_id_type=MESH
        )
    load = pltpu.make_async_copy(sens_hbm, sens, sens_sem)
    load.start()
    gath[stn] = controls[...]
    pl.semaphore_wait(barrier, len(everyone))

    listed = [[margin[blocks[n], o] for o in range(MARGINS)] for n in range(SLOTS)]
    entry = lax.broadcasted_iota(jnp.int32, (SLOTS * MARGINS, MEMBERS), 0)
    lists = jnp.zeros((SLOTS * MARGINS, MEMBERS), F32)
    for n in range(SLOTS):
        for o in range(MARGINS):
            lists = jnp.where(entry == n * MARGINS + o, listed[n][o].astype(F32), lists)
    list_in[stn] = lists

    for peer in z_peers:
        send(gath.at[stn], gath.at[stn], gz_s, gz_r, peer)
    for peer in s_peers:
        send(list_in.at[stn], list_in.at[stn], li_s, li_r, peer)

    lane = lax.broadcasted_iota(jnp.int32, (8, MEMBERS), 1)
    rows_of_centres = [
        jnp.broadcast_to(centres[0:1, i * MEMBERS:(i + 1) * MEMBERS], (8, MEMBERS)) for i in range(8)
    ]
    to_row = lax.broadcasted_iota(jnp.int32, (MEMBERS, MEMBERS), 0)
    to_col = lax.broadcasted_iota(jnp.int32, (MEMBERS, MEMBERS), 1)
    by_row = (to_row == (to_col % MARGINS) * CENTRES + to_col // MARGINS).astype(BF16)
    for n in range(SLOTS):
        block = blocks[n]
        centre = jnp.zeros((8, MEMBERS), jnp.int32)
        for o in range(MARGINS):
            j = listed[n][o]
            row = rows_of_centres[0]
            for i in range(1, 8):
                row = jnp.where(j // 4 == i, rows_of_centres[i], row)
            turned = row
            for i in range(1, 4):
                turned = jnp.where((o + 4 - j % 4) % 4 == i, pltpu.roll(row, i * CENTRES, 1), turned)
            centre = jnp.where(lane // CENTRES == o, turned, centre)
        centre = centre[0:1]
        cells = lax.broadcasted_iota(jnp.int32, (BLOCK, MEMBERS), 0) + block * BLOCK
        squared = jnp.zeros((BLOCK, MEMBERS), F32)
        for shift, mask in ((10, 1048575), (5, 31), (0, 31)):
            cell_coord = ((cells >> shift) & mask).astype(F32)
            centre_coord = ((centre >> shift) & mask).astype(F32)
            spread = cell_coord - centre_coord
            squared = squared + spread * spread
        table = jnp.exp(squared * (-0.5 / 100.0))
        high, low = split(table)
        basis[n, :, 0:MEMBERS] = high
        basis[n, :, MEMBERS:] = low
        high = jnp.dot(high, by_row, preferred_element_type=F32)
        low = jnp.dot(low, by_row, preferred_element_type=F32)
        basis_r[n, :, 0:MEMBERS] = high.astype(BF16)
        basis_r[n, :, MEMBERS:] = low.astype(BF16)
        basis_t[n, 0:MEMBERS] = high.T.astype(BF16)
        basis_t[n, MEMBERS:] = low.T.astype(BF16)

    drain(gath.at[0:NZ - 1], gz_r)
    x_rows = pl.ds(x * NZ, NZ)
    for peer in x_peers:
        send(gath.at[x_rows], gath.at[x_rows], gx_s, gx_r, peer)
    load.wait()
    for n in range(SLOTS):
        for i in range(4):
            piece = sens[n, i * 128:(i + 1) * 128, :]
            sens_t[n, :, i * 128:(i + 1) * 128] = piece.T
    drain(list_in.at[0:NSTN - 1], li_r)
    flat_lists = list_in[...].reshape(NSTN * SLOTS * MARGINS, MEMBERS)
    found = (flat_lists == lax.broadcasted_iota(jnp.int32, flat_lists.shape, 1).astype(F32)).astype(F32)
    hot[...] = found.astype(BF16)
    hot_t[...] = found.T[0:NSTN].astype(BF16)
    grad_rhs[...] = jnp.zeros_like(grad_rhs)
    drain(gath.at[0:NSTN - NZ], gx_r)

    def times_basis(table, n):
        both = jnp.dot(table[n], coeff_rhs[n], preferred_element_type=F32)
        return both[:, 0:MEMBERS] + both[:, MEMBERS:]

    def put_coeffs(n, at, rows, value):
        high, low = split(value)
        for base in (0, MEMBERS):
            coeff_rhs[n, base + at:base + at + rows, 0:MEMBERS] = high
            coeff_rhs[n, base + at:base + at + rows, MEMBERS:] = low

    def both_ways(left, rhs):
        both = jnp.dot(left, rhs, preferred_element_type=F32)
        return both[:, 0:MEMBERS] + both[:, MEMBERS:]

    def station(k):
        both = jnp.dot(sens[0], cell_rhs[0], preferred_element_type=F32)
        both += jnp.dot(sens[1], cell_rhs[1], preferred_element_type=F32)
        part[k] = (both[:, 0:MEMBERS] + both[:, MEMBERS:]).reshape(NCELL // 2, 2, CENTRES, MEMBERS)

    def put_cells(n, value):
        high, low = split(value)
        cell_rhs[n, :, 0:MEMBERS] = high
        cell_rhs[n, :, MEMBERS:] = low

    def sum_cells(k, group_norm=None):
        send(part.at[k, :, 1 - core], core_in.at[k], c_s.at[k], c_r.at[k], core_peer)
        if group_norm is not None:
            row_core[k] = group_norm()
            send(row_core.at[k], row_core_in.at[k], rc_s.at[k], rc_r.at[k], core_peer)
        drain(core_in.at[k], c_r.at[k])
        paired[k] = part[k, :, core] + core_in[k]
        for peer in y_peers:
            send(paired.at[k, peer[0]], y_in.at[k, y], y_s.at[k], y_r.at[k], peer)
        y_in[k, y] = paired[k, y]
        norm = None
        if group_norm is not None:
            drain(row_core_in.at[k], rc_r.at[k])
            row_y[k] = row_core[k] + row_core_in[k]
            for peer in y_peers:
                send(row_y.at[k], row_y_in.at[k, y], ry_s.at[k], ry_r.at[k], peer)
            row_y_in[k, y] = row_y[k]
            drain(row_y_in.at[k, 0:NY - 1], ry_r.at[k])
            norm = sum(row_y_in[k, i] for i in range(NY))
        drain(y_in.at[k, 0:NY - 1], y_r.at[k])
        return sum(y_in[k, i] for i in range(NY)), norm

    def gather_cells(k, rows):
        full[k, y, core] = rows
        for peer in y_peers:
            send(full.at[k, y, core], full.at[k, y, core], fy_s.at[k], fy_r.at[k], peer)
        drain(full.at[k, 0:NY - 1, 0], fy_r.at[k])
        send(full.at[k, :, core], full.at[k, :, core], fc_s.at[k], fc_r.at[k], core_peer)
        drain(full.at[k, :, 0], fc_r.at[k])

    def adjoint(k, with_curvature):
        rows = full[k].reshape(BLOCK, MEMBERS)
        if with_curvature:
            row_s[k] = column_sum(rows * rows)
            for peer in s_peers:
                send(row_s.at[k], row_s_in.at[k, stn], rs_s.at[k], rs_r.at[k], peer)
            row_s_in[k, stn] = row_s[k]
        high, low = split(rows)
        row_rhs[:, 0:MEMBERS] = high
        row_rhs[:, MEMBERS:] = low
        parts = []
        for n in range(SLOTS):
            put_cells(n, slope[n] * both_ways(sens_t[n], row_rhs[...]))
            two = both_ways(basis_t[n], cell_rhs[n])
            parts.append((two[0:MEMBERS] + two[MEMBERS:]).reshape(CENTRES // 2, 2 * MARGINS, MEMBERS))
        even, odd = interleave(parts[0], parts[1])
        scat_out[k, :, 0] = even
        scat_out[k, :, 1] = odd
        for peer in s_peers:
            send(scat_out.at[k, peer[0] // 2, peer[0] % 2], scat_in.at[k, stn], sc_s.at[k], sc_r.at[k], peer)
        scat_in[k, stn] = scat_out[k, stn // 2, stn % 2]
        curvature = None
        if with_curvature:
            drain(row_s_in.at[k, 0:NSTN - 1], rs_r.at[k])
            curvature = sum(row_s_in[k, i] for i in range(NSTN))
        drain(scat_in.at[k, 0:NSTN - 1], sc_r.at[k])
        high, low = split(scat_in[k].reshape(NSTN * SLOTS * MARGINS, MEMBERS))
        entry_rhs[:, 0:MEMBERS] = high
        entry_rhs[:, MEMBERS:] = low
        return both_ways(hot_t[...], entry_rhs[...]), curvature

    def answer(k):
        high, low = split(own_grad[...])
        grad_rhs[0:NSTN, 0:MEMBERS] = high
        grad_rhs[0:NSTN, MEMBERS:] = low
        ans_out[k] = both_ways(hot[...], grad_rhs[...]).reshape(NSTN, SLOTS * MARGINS, MEMBERS)
        for peer in s_peers:
            send(ans_out.at[k, peer[0]], ans_in.at[k, stn], an_s.at[k], an_r.at[k], peer)
        ans_in[k, stn] = ans_out[k, stn]
        own = own_grad[...]
        square = column_sum(own * own)
        for j in range(NSTN):
            pair_out[k, j, 0:1] = own[j:j + 1]
            pair_out[k, j, 1:2] = square
        for peer in s_peers:
            send(pair_out.at[k, peer[0]], pair_in.at[k, stn], pr_s.at[k], pr_r.at[k], peer)
        pair_in[k, stn] = pair_out[k, stn]

    for n in range(SLOTS):
        for o in range(MARGINS):
            put_coeffs(n, o * CENTRES, CENTRES, gath[listed[n][o]])
        tanh_phi = jnp.tanh(times_basis(basis, n))
        slope[n] = 0.5 * (1.0 - tanh_phi * tanh_phi)
        put_cells(n, 0.5 * (1.0 + tanh_phi))
    station(0)
    predicted, _ = sum_cells(0)
    own_res[...] = observed[...] - predicted
    gather_cells(0, own_res[...])
    gradient, _ = adjoint(0, False)
    own_grad[...] = gradient

    norm = None
    for k in range(1, ITERS + 1):
        answer(k - 1)
        drain(ans_in.at[k - 1, 0:NSTN - 1], an_r.at[k - 1])
        tiles = ans_in[k - 1].reshape(CENTRES // 2, 2, SLOTS * MARGINS, MEMBERS)
        for n, tile in enumerate(interleave(tiles[:, 0], tiles[:, 1])):
            put_coeffs(n, 0, MEMBERS, tile.reshape(MEMBERS, MEMBERS))
            put_cells(n, slope[n] * times_basis(basis_r, n))
        station(k)

        def group_norm():
            drain(pair_in.at[k - 1, 0:NSTN - 1], pr_r.at[k - 1])
            return sum(pair_in[k - 1, i, 1:2] for i in range(NSTN))

        image, new_norm = sum_cells(k, group_norm)
        direction = jnp.concatenate([pair_in[k - 1, i, 0:1] for i in range(NSTN)], axis=0)
        if k > 1:
            ratio = new_norm / norm
            image = image + ratio * own_image[...]
            direction = direction + ratio * own_dir[...]
        norm = new_norm
        own_image[...] = image
        own_dir[...] = direction
        if k < ITERS:
            gather_cells(k, image)
            change, curvature = adjoint(k, True)
            step = norm / curvature
            own_grad[...] = own_grad[...] - step * change
        else:
            row_core[0] = column_sum(image * image)
            send(row_core.at[0], row_core_in.at[0], rc_s.at[0], rc_r.at[0], core_peer)
            drain(row_core_in.at[0], rc_r.at[0])
            row_y[0] = row_core[0] + row_core_in[0]
            for peer in y_peers:
                send(row_y.at[0], row_y_in.at[0, y], ry_s.at[0], ry_r.at[0], peer)
            row_y_in[0, y] = row_y[0]
            drain(row_y_in.at[0, 0:NY - 1], ry_r.at[0])
            row_s[0] = sum(row_y_in[0, i] for i in range(NY))
            for peer in s_peers:
                send(row_s.at[0], row_s_in.at[0, stn], rs_s.at[0], rs_r.at[0], peer)
            row_s_in[0, stn] = row_s[0]
            drain(row_s_in.at[0, 0:NSTN - 1], rs_r.at[0])
            step = norm / sum(row_s_in[0, i] for i in range(NSTN))
        own_res[...] = own_res[...] - step * image
        own_upd[...] = step * direction if k == 1 else own_upd[...] + step * direction

    updated[...] = controls[...] + own_upd[...]
    final_residual[...] = own_res[...]

    drain(gath.at[0:NZ - 1], gz_s)
    drain(gath.at[0:NSTN - NZ], gx_s)
    drain(list_in.at[0:NSTN - 1], li_s)
    for k in range(ITERS + 1):
        drain(core_in.at[k], c_s.at[k])
        drain(y_in.at[k, 0:NY - 1], y_s.at[k])
        drain(row_core_in.at[k], rc_s.at[k])
        drain(row_y_in.at[k, 0:NY - 1], ry_s.at[k])
    for k in range(ITERS):
        drain(full.at[k, 0:NY - 1, 0], fy_s.at[k])
        drain(full.at[k, :, 0], fc_s.at[k])
        drain(scat_in.at[k, 0:NSTN - 1], sc_s.at[k])
        drain(ans_in.at[k, 0:NSTN - 1], an_s.at[k])
        drain(row_s_in.at[k, 0:NSTN - 1], rs_s.at[k])
        drain(pair_in.at[k, 0:NSTN - 1], pr_s.at[k])


def local(sensitivity, block_list, margin, centres, controls, observed):
    rows = (CENTRES, MEMBERS)
    a, d = ITERS + 1, ITERS

    def vmem(*shape):
        return pltpu.VMEM(shape, F32)

    entries = SLOTS * MARGINS
    scratch = [
        pltpu.VMEM((SLOTS, BLOCK, BLOCK), BF16),
        pltpu.VMEM((SLOTS, BLOCK, BLOCK), BF16),
        pltpu.VMEM((SLOTS, BLOCK, 2 * MEMBERS), BF16),
        pltpu.VMEM((SLOTS, BLOCK, 2 * MEMBERS), BF16),
        pltpu.VMEM((SLOTS, 2 * MEMBERS, BLOCK), BF16),
        pltpu.VMEM((SLOTS, 2 * MEMBERS, 2 * MEMBERS), BF16),
        pltpu.VMEM((SLOTS, BLOCK, 2 * MEMBERS), BF16),
        pltpu.VMEM((BLOCK, 2 * MEMBERS), BF16),
        vmem(SLOTS, BLOCK, MEMBERS),
        vmem(NSTN, entries, MEMBERS),
        pltpu.VMEM((NSTN * entries, MEMBERS), BF16),
        pltpu.VMEM((NSTN, NSTN * entries), BF16),
        pltpu.VMEM((MEMBERS, 2 * MEMBERS), BF16),
        pltpu.VMEM((NSTN * entries, 2 * MEMBERS), BF16),
        vmem(NSTN, *rows),
        vmem(a, NY, 2, *rows),
        vmem(a, NY, *rows),
        vmem(a, NY, *rows),
        vmem(a, NY, *rows),
        vmem(d, NY, 2, *rows),
        vmem(d, CENTRES // 2, 2, entries, MEMBERS),
        vmem(d, NSTN, entries, MEMBERS),
        vmem(d, NSTN, entries, MEMBERS),
        vmem(d, NSTN, entries, MEMBERS),
        vmem(*rows), vmem(*rows), vmem(*rows), vmem(*rows), vmem(*rows),
        vmem(a, 1, MEMBERS), vmem(a, 1, MEMBERS),
        vmem(a, 1, MEMBERS), vmem(a, NY, 1, MEMBERS),
        vmem(d, 1, MEMBERS), vmem(d, NSTN, 1, MEMBERS),
        vmem(d, NSTN, 2, MEMBERS), vmem(d, NSTN, 2, MEMBERS),
    ]
    scratch += [pltpu.SemaphoreType.DMA] * 7
    scratch += [pltpu.SemaphoreType.DMA((a,))] * 4
    scratch += [pltpu.SemaphoreType.DMA((d,))] * 8
    scratch += [pltpu.SemaphoreType.DMA((a,))] * 4
    scratch += [pltpu.SemaphoreType.DMA((d,))] * 4
    in_vmem = pl.BlockSpec(memory_space=pltpu.VMEM)
    in_smem = pl.BlockSpec(memory_space=pltpu.SMEM)
    return pl.pallas_call(
        kernel,
        out_shape=(jax.ShapeDtypeStruct(rows, F32), jax.ShapeDtypeStruct(rows, F32)),
        in_specs=[pl.BlockSpec(memory_space=pl.ANY), in_smem, in_smem, in_vmem, in_vmem, in_vmem],
        out_specs=(in_vmem, in_vmem),
        scratch_shapes=scratch,
        compiler_params=pltpu.CompilerParams(
            collective_id=0, has_side_effects=True, vmem_limit_bytes=40 * 1024 * 1024
        ),
        cost_estimate=pl.CostEstimate(flops=3_000_000_000, bytes_accessed=2_000_000, transcendentals=262144),
        name="gauss_newton",
    )(
        sensitivity.reshape(SLOTS, BLOCK, BLOCK), block_list.reshape(SLOTS), margin, centres,
        controls, observed,
    )


def solution(mesh):
    return jax.shard_map(
        local,
        mesh=mesh,
        in_specs=(
            P("stn", "cell", None, None, None),
            P("stn", "cell", None),
            P("cell", None),
            P("cell", None),
            P(("stn", "cell"), None),
            P(("stn", "cell"), None),
        ),
        out_specs=(P(("stn", "cell"), None), P(("stn", "cell"), None)),
        check_vma=False,
    )
```

```python
import jax
import jax.numpy as jnp
from jax import lax
from jax.experimental import pallas as pl
from jax.experimental.pallas import tpu as pltpu
from jax.sharding import PartitionSpec as P

MESH = pl.DeviceIdType.MESH
ITERS = 3
SLOTS, BLOCK, MARGINS, CENTRES, MEMBERS = 2, 512, 4, 32, 128
NX, NZ, NY = 4, 8, 8
NSTN, NCELL = NX * NZ, NY * 2
F32, BF16 = jnp.float32, jnp.bfloat16


def split(value):
    high = value.astype(BF16)
    low = (value - high.astype(F32)).astype(BF16)
    return high, low


def column_sum(value):
    return jnp.sum(value.reshape(-1, MEMBERS), axis=0, keepdims=True)


def interleave(first, second):
    upper = lax.broadcasted_iota(jnp.int32, first.shape, 1) < MARGINS
    even = jnp.where(upper, first, pltpu.roll(second, MARGINS, 1))
    odd = jnp.where(upper, pltpu.roll(first, MARGINS, 1), second)
    return even, odd


def kernel(
    sens_hbm, blocks, margin, centres, controls, observed, updated, final_residual,
    sens, sens_t, basis, basis_r, basis_t, coeff_rhs, cell_rhs, row_rhs, slope,
    list_in, hot, hot_t, same, entry_rhs,
    gath, part, core_in, paired, y_in, full, scat_out, scat_in, ans_out, ans_in,
    own_grad, own_dir, own_image, own_res, own_upd,
    row_core, row_core_in, row_y, row_y_in, row_s, row_s_in, row_c, row_c_in, pair_out, pair_in,
    sens_sem, li_s, li_r, gz_s, gz_r, gx_s, gx_r, hx_s, hx_r, hz_s, hz_r, cc_s, cc_r,
    c_s, c_r, y_s, y_r, fy_s, fy_r, fc_s, fc_r,
    sc_s, sc_r, an_s, an_r, rc_s, rc_r, ry_s, ry_r, rs_s, rs_r, pr_s, pr_r,
):
    stn, cell = lax.axis_index("stn"), lax.axis_index("cell")
    x, z = stn // NZ, stn % NZ
    y, core = cell // 2, cell % 2
    def ring(size, step):
        return min(step, size - step)

    far_y = sorted(range(1, NY), key=lambda d: -ring(NY, d))
    far_z = sorted(range(1, NZ), key=lambda d: -ring(NZ, d))
    far_x = sorted(range(1, NX), key=lambda d: -ring(NX, d))
    far_s = sorted(
        [(a, b) for a in range(NX) for b in range(NZ) if a or b],
        key=lambda d: -ring(NX, d[0]) - ring(NZ, d[1]),
    )
    x_peers = [((x + d) % NX, ((x + d) % NX) * NZ + z, cell) for d in far_x]
    z_peers = [((z + d) % NZ, x * NZ + (z + d) % NZ, cell) for d in far_z]
    y_peers = [((y + d) % NY, stn, ((y + d) % NY) * 2 + core) for d in far_y]
    y_others = [((y + d) % NY, stn, ((y + d) % NY) * 2 + 1 - core) for d in far_y]
    core_peer = (1 - core, stn, y * 2 + 1 - core)
    s_peers = [((x + a) % NX * NZ + (z + b) % NZ, (x + a) % NX * NZ + (z + b) % NZ, cell) for a, b in far_s]

    def send(src, dst, ssem, rsem, peer):
        pltpu.make_async_remote_copy(
            src_ref=src, dst_ref=dst, send_sem=ssem, recv_sem=rsem,
            device_id={"stn": peer[1], "cell": peer[2]}, device_id_type=MESH,
        ).start()

    def drain(ref, sem):
        pltpu.make_async_copy(ref, ref, sem).wait()

    barrier = pltpu.get_barrier_semaphore()
    everyone = s_peers + y_peers + y_others + [core_peer]
    for peer in everyone:
        pl.semaphore_signal(
            barrier, inc=1, device_id={"stn": peer[1], "cell": peer[2]}, device_id_type=MESH
        )
    loads = [
        pltpu.make_async_copy(sens_hbm.at[n, :, side], sens.at[half, n], sens_sem.at[half * SLOTS + n])
        for half, side in ((0, 1 - core), (1, core)) for n in range(SLOTS)
    ]
    for load in loads:
        load.start()
    gath[x, z] = controls[...]
    pl.semaphore_wait(barrier, len(everyone))

    most, rest = pl.ds(0, 24), pl.ds(24, 8)
    for peer in z_peers:
        send(gath.at[x, z, most], gath.at[x, z, most], gz_s, gz_r, peer)
    for peer in x_peers:
        send(gath.at[x, z, rest], gath.at[x, z, rest], hx_s, hx_r, peer)

    listed = [[margin[o, blocks[n]] for o in range(MARGINS)] for n in range(SLOTS)]
    entry = lax.broadcasted_iota(jnp.int32, (SLOTS * MARGINS, MEMBERS), 0)
    lists = jnp.zeros((SLOTS * MARGINS, MEMBERS), F32)
    for n in range(SLOTS):
        for o in range(MARGINS):
            lists = jnp.where(entry == n * MARGINS + o, listed[n][o].astype(F32), lists)
    list_in[stn] = lists

    lane = lax.broadcasted_iota(jnp.int32, (8, MEMBERS), 1)
    rows_of_centres = [
        jnp.broadcast_to(centres[0:1, i * MEMBERS:(i + 1) * MEMBERS], (8, MEMBERS)) for i in range(8)
    ]
    to_row = lax.broadcasted_iota(jnp.int32, (MEMBERS, MEMBERS), 0)
    to_col = lax.broadcasted_iota(jnp.int32, (MEMBERS, MEMBERS), 1)
    by_row = (to_row == (to_col % MARGINS) * CENTRES + to_col // MARGINS).astype(BF16)
    for n in range(SLOTS):
        block = blocks[n]
        centre = jnp.zeros((8, MEMBERS), jnp.int32)
        for o in range(MARGINS):
            j = listed[n][o]
            row = rows_of_centres[0]
            for i in range(1, 8):
                row = jnp.where(j // 4 == i, rows_of_centres[i], row)
            turned = row
            for i in range(1, 4):
                turned = jnp.where((o + 4 - j % 4) % 4 == i, pltpu.roll(row, i * CENTRES, 1), turned)
            centre = jnp.where(lane // CENTRES == o, turned, centre)
        centre = centre[0:1]
        cells = lax.broadcasted_iota(jnp.int32, (BLOCK, MEMBERS), 0) + block * BLOCK
        squared = jnp.zeros((BLOCK, MEMBERS), F32)
        for shift, mask in ((10, 1048575), (5, 31), (0, 31)):
            cell_coord = ((cells >> shift) & mask).astype(F32)
            centre_coord = ((centre >> shift) & mask).astype(F32)
            spread = cell_coord - centre_coord
            squared = squared + spread * spread
        table = jnp.exp(squared * (-0.5 / 100.0))
        high, low = split(table)
        basis[n, :, 0:MEMBERS] = high
        basis[n, :, MEMBERS:] = low
        high = jnp.dot(high, by_row, preferred_element_type=F32)
        low = jnp.dot(low, by_row, preferred_element_type=F32)
        basis_r[n, :, 0:MEMBERS] = high.astype(BF16)
        basis_r[n, :, MEMBERS:] = low.astype(BF16)
        basis_t[n, 0:MEMBERS] = high.T.astype(BF16)
        basis_t[n, MEMBERS:] = low.T.astype(BF16)

    drain(gath.at[0, 0:NZ - 1, most], gz_r)
    for peer in x_peers:
        send(gath.at[x, :, most], gath.at[x, :, most], gx_s, gx_r, peer)
    drain(gath.at[0:NX - 1, 0, rest], hx_r)
    for peer in z_peers:
        send(gath.at[:, z, rest], gath.at[:, z, rest], hz_s, hz_r, peer)
    for load in loads:
        load.wait()
    for half in range(2):
        for n in range(SLOTS):
            for i in range(2):
                piece = sens[half, n, i * 4:(i + 1) * 4].reshape(128, BLOCK)
                sens_t[half, n, :, i * 128:(i + 1) * 128] = piece.T
    drain(gath.at[0:NX - 1, :, most], gx_r)
    drain(gath.at[:, 0:NZ - 1, rest], hz_r)

    def send_lists():
        for peer in s_peers:
            send(list_in.at[stn], list_in.at[stn], li_s, li_r, peer)

    def use_lists():
        drain(list_in.at[0:NSTN - 1], li_r)
        flat_lists = list_in[...].reshape(NSTN * SLOTS * MARGINS, MEMBERS)
        found = (flat_lists == lax.broadcasted_iota(jnp.int32, flat_lists.shape, 1).astype(F32)).astype(F32)
        hot[...] = found.astype(BF16)
        found_t = found.T.astype(BF16)
        hot_t[...] = found_t[0:NSTN]
        same[...] = jnp.dot(hot[...], found_t, preferred_element_type=F32).astype(BF16)

    def times_basis(table, n):
        both = jnp.dot(table[n], coeff_rhs[n], preferred_element_type=F32)
        return both[:, 0:MEMBERS] + both[:, MEMBERS:]

    def put_coeffs(n, at, rows, value):
        high, low = split(value)
        for base in (0, MEMBERS):
            coeff_rhs[n, base + at:base + at + rows, 0:MEMBERS] = high
            coeff_rhs[n, base + at:base + at + rows, MEMBERS:] = low

    def both_ways(left, rhs):
        both = jnp.dot(left, rhs, preferred_element_type=F32)
        return both[:, 0:MEMBERS] + both[:, MEMBERS:]

    def station_rows(half):
        both = jnp.dot(sens[half, 0].reshape(BLOCK // 2, BLOCK), cell_rhs[0], preferred_element_type=F32)
        both += jnp.dot(sens[half, 1].reshape(BLOCK // 2, BLOCK), cell_rhs[1], preferred_element_type=F32)
        return (both[:, 0:MEMBERS] + both[:, MEMBERS:]).reshape(NY, CENTRES, MEMBERS)

    def put_cells(n, value):
        high, low = split(value)
        cell_rhs[n, :, 0:MEMBERS] = high
        cell_rhs[n, :, MEMBERS:] = low

    def sum_cells(k, group_norm=None, meanwhile=None):
        part[k] = station_rows(0)
        send(part.at[k], core_in.at[k], c_s.at[k], c_r.at[k], core_peer)
        own_rows = station_rows(1)
        if group_norm is not None:
            row_core[k] = group_norm()
            send(row_core.at[k], row_core_in.at[k], rc_s.at[k], rc_r.at[k], core_peer)
        drain(core_in.at[k], c_r.at[k])
        paired[k] = own_rows + core_in[k]
        for peer in y_peers:
            send(paired.at[k, peer[0]], y_in.at[k, y], y_s.at[k], y_r.at[k], peer)
        y_in[k, y] = paired[k, y]
        if meanwhile is not None:
            meanwhile()
        norm = None
        if group_norm is not None:
            drain(row_core_in.at[k], rc_r.at[k])
            row_y[k] = row_core[k] + row_core_in[k]
            for peer in y_peers:
                send(row_y.at[k], row_y_in.at[k, y], ry_s.at[k], ry_r.at[k], peer)
            row_y_in[k, y] = row_y[k]
            drain(row_y_in.at[k, 0:NY - 1], ry_r.at[k])
            norm = sum(row_y_in[k, i] for i in range(NY))
        drain(y_in.at[k, 0:NY - 1], y_r.at[k])
        return sum(y_in[k, i] for i in range(NY)), norm

    def gather_cells(k, rows):
        full[k, 1, y] = rows
        for peer in y_peers:
            send(full.at[k, 1, y], full.at[k, 1, y], fy_s.at[k], fy_r.at[k], peer)

    def pull(k, half, n):
        return both_ways(sens_t[half, n], row_rhs[half])

    def put_rows(half, value):
        high, low = split(value)
        row_rhs[half, :, 0:MEMBERS] = high
        row_rhs[half, :, MEMBERS:] = low

    def adjoint(k, with_curvature):
        drain(full.at[k, 1, 0:NY - 1], fy_r.at[k])
        send(full.at[k, 1], full.at[k, 0], fc_s.at[k], fc_r.at[k], core_peer)
        own_rows = full[k, 1].reshape(BLOCK // 2, MEMBERS)
        put_rows(1, own_rows)
        pulled = [pull(k, 1, n) for n in range(SLOTS)]
        squares = column_sum(own_rows * own_rows)
        drain(full.at[k, 0], fc_r.at[k])
        rows = full[k, 0].reshape(BLOCK // 2, MEMBERS)
        if with_curvature:
            row_s[k] = squares + column_sum(rows * rows)
            for peer in s_peers:
                send(row_s.at[k], row_s_in.at[k, stn], rs_s.at[k], rs_r.at[k], peer)
            row_s_in[k, stn] = row_s[k]
        put_rows(0, rows)
        parts = []
        for n in range(SLOTS):
            put_cells(n, slope[n] * (pulled[n] + pull(k, 0, n)))
            two = both_ways(basis_t[n], cell_rhs[n])
            parts.append((two[0:MEMBERS] + two[MEMBERS:]).reshape(CENTRES // 2, 2 * MARGINS, MEMBERS))
        even, odd = interleave(parts[0], parts[1])
        scat_out[k, :, 0] = even
        scat_out[k, :, 1] = odd
        for peer in s_peers:
            send(scat_out.at[k, peer[0] // 2, peer[0] % 2], scat_in.at[k, stn], sc_s.at[k], sc_r.at[k], peer)
        scat_in[k, stn] = scat_out[k, stn // 2, stn % 2]
        curvature = None
        if with_curvature:
            drain(row_s_in.at[k, 0:NSTN - 1], rs_r.at[k])
            curvature = sum(row_s_in[k, i] for i in range(NSTN))
        drain(scat_in.at[k, 0:NSTN - 1], sc_r.at[k])
        high, low = split(scat_in[k].reshape(NSTN * SLOTS * MARGINS, MEMBERS))
        entry_rhs[:, 0:MEMBERS] = high
        entry_rhs[:, MEMBERS:] = low
        return curvature

    def own_change():
        return both_ways(hot_t[...], entry_rhs[...])

    def answer(k, step=None):
        change = both_ways(same[...], entry_rhs[...]).reshape(NSTN, SLOTS * MARGINS, MEMBERS)
        ans_out[k] = change if step is None else ans_out[k - 1] - step * change
        for peer in s_peers:
            send(ans_out.at[k, peer[0]], ans_in.at[k, stn], an_s.at[k], an_r.at[k], peer)
        ans_in[k, stn] = ans_out[k, stn]
        own = own_change() if step is None else own_grad[...] - step * own_change()
        own_grad[...] = own
        square = column_sum(own * own)
        for j in range(NSTN):
            pair_out[k, j, 0:1] = own[j:j + 1]
            pair_out[k, j, 1:2] = square
        for peer in s_peers:
            send(pair_out.at[k, peer[0]], pair_in.at[k, stn], pr_s.at[k], pr_r.at[k], peer)
        pair_in[k, stn] = pair_out[k, stn]

    for n in range(SLOTS):
        for o in range(MARGINS):
            put_coeffs(n, o * CENTRES, CENTRES, gath[listed[n][o] // NZ, listed[n][o] % NZ])
        tanh_phi = jnp.tanh(times_basis(basis, n))
        slope[n] = 0.5 * (1.0 - tanh_phi * tanh_phi)
        put_cells(n, 0.5 * (1.0 + tanh_phi))
    predicted, _ = sum_cells(0, meanwhile=send_lists)
    own_res[...] = observed[...] - predicted
    gather_cells(0, own_res[...])
    use_lists()
    adjoint(0, False)
    answer(0)

    norm = None
    for k in range(1, ITERS + 1):
        drain(ans_in.at[k - 1, 0:NSTN - 1], an_r.at[k - 1])
        tiles = ans_in[k - 1].reshape(CENTRES // 2, 2, SLOTS * MARGINS, MEMBERS)
        for n, tile in enumerate(interleave(tiles[:, 0], tiles[:, 1])):
            put_coeffs(n, 0, MEMBERS, tile.reshape(MEMBERS, MEMBERS))
            put_cells(n, slope[n] * times_basis(basis_r, n))

        def group_norm():
            drain(pair_in.at[k - 1, 0:NSTN - 1], pr_r.at[k - 1])
            return sum(pair_in[k - 1, i, 1:2] for i in range(NSTN))

        image, new_norm = sum_cells(k, group_norm)
        direction = jnp.concatenate([pair_in[k - 1, i, 0:1] for i in range(NSTN)], axis=0)
        if k > 1:
            ratio = new_norm / norm
            image = image + ratio * own_image[...]
            direction = direction + ratio * own_dir[...]
        norm = new_norm
        own_image[...] = image
        own_dir[...] = direction
        if k < ITERS:
            gather_cells(k, image)
            curvature = adjoint(k, True)
            step = norm / curvature
            answer(k, step)
        else:
            row_c[...] = column_sum(image * image)
            for peer in y_others + y_peers + [core_peer]:
                send(row_c, row_c_in.at[cell], cc_s, cc_r, peer)
            row_c_in[cell] = row_c[...]
            drain(row_c_in.at[0:NCELL - 1], cc_r)
            row_s[0] = sum(row_c_in[i] for i in range(NCELL))
            for peer in s_peers:
                send(row_s.at[0], row_s_in.at[0, stn], rs_s.at[0], rs_r.at[0], peer)
            row_s_in[0, stn] = row_s[0]
            drain(row_s_in.at[0, 0:NSTN - 1], rs_r.at[0])
            step = norm / sum(row_s_in[0, i] for i in range(NSTN))
        own_res[...] = own_res[...] - step * image
        own_upd[...] = step * direction if k == 1 else own_upd[...] + step * direction

    updated[...] = controls[...] + own_upd[...]
    final_residual[...] = own_res[...]

    drain(gath.at[0, 0:NZ - 1, most], gz_s)
    drain(gath.at[0:NX - 1, :, most], gx_s)
    drain(gath.at[0:NX - 1, 0, rest], hx_s)
    drain(gath.at[:, 0:NZ - 1, rest], hz_s)
    drain(row_c_in.at[0:NCELL - 1], cc_s)
    drain(list_in.at[0:NSTN - 1], li_s)
    for k in range(ITERS + 1):
        drain(core_in.at[k], c_s.at[k])
        drain(y_in.at[k, 0:NY - 1], y_s.at[k])
    for k in range(1, ITERS + 1):
        drain(row_core_in.at[k], rc_s.at[k])
        drain(row_y_in.at[k, 0:NY - 1], ry_s.at[k])
    for k in range(ITERS):
        drain(full.at[k, 1, 0:NY - 1], fy_s.at[k])
        drain(full.at[k, 1], fc_s.at[k])
        drain(scat_in.at[k, 0:NSTN - 1], sc_s.at[k])
        drain(ans_in.at[k, 0:NSTN - 1], an_s.at[k])
        drain(row_s_in.at[k, 0:NSTN - 1], rs_s.at[k])
        drain(pair_in.at[k, 0:NSTN - 1], pr_s.at[k])


def local(sensitivity, block_list, margin, centres, controls, observed):
    rows = (CENTRES, MEMBERS)
    a, d = ITERS + 1, ITERS

    def vmem(*shape):
        return pltpu.VMEM(shape, F32)

    entries = SLOTS * MARGINS
    scratch = [
        pltpu.VMEM((2, SLOTS, NY, CENTRES, BLOCK), BF16),
        pltpu.VMEM((2, SLOTS, BLOCK, BLOCK // 2), BF16),
        pltpu.VMEM((SLOTS, BLOCK, 2 * MEMBERS), BF16),
        pltpu.VMEM((SLOTS, BLOCK, 2 * MEMBERS), BF16),
        pltpu.VMEM((SLOTS, 2 * MEMBERS, BLOCK), BF16),
        pltpu.VMEM((SLOTS, 2 * MEMBERS, 2 * MEMBERS), BF16),
        pltpu.VMEM((SLOTS, BLOCK, 2 * MEMBERS), BF16),
        pltpu.VMEM((2, BLOCK // 2, 2 * MEMBERS), BF16),
        vmem(SLOTS, BLOCK, MEMBERS),
        vmem(NSTN, entries, MEMBERS),
        pltpu.VMEM((NSTN * entries, MEMBERS), BF16),
        pltpu.VMEM((NSTN, NSTN * entries), BF16),
        pltpu.VMEM((NSTN * entries, NSTN * entries), BF16),
        pltpu.VMEM((NSTN * entries, 2 * MEMBERS), BF16),
        vmem(NX, NZ, *rows),
        vmem(a, NY, *rows),
        vmem(a, NY, *rows),
        vmem(a, NY, *rows),
        vmem(a, NY, *rows),
        vmem(d, 2, NY, *rows),
        vmem(d, CENTRES // 2, 2, entries, MEMBERS),
        vmem(d, NSTN, entries, MEMBERS),
        vmem(d, NSTN, entries, MEMBERS),
        vmem(d, NSTN, entries, MEMBERS),
        vmem(*rows), vmem(*rows), vmem(*rows), vmem(*rows), vmem(*rows),
        vmem(a, 1, MEMBERS), vmem(a, 1, MEMBERS),
        vmem(a, 1, MEMBERS), vmem(a, NY, 1, MEMBERS),
        vmem(d, 1, MEMBERS), vmem(d, NSTN, 1, MEMBERS),
        vmem(1, MEMBERS), vmem(NCELL, 1, MEMBERS),
        vmem(d, NSTN, 2, MEMBERS), vmem(d, NSTN, 2, MEMBERS),
    ]
    scratch += [pltpu.SemaphoreType.DMA((2 * SLOTS,))]
    scratch += [pltpu.SemaphoreType.DMA] * 12
    scratch += [pltpu.SemaphoreType.DMA((a,))] * 4
    scratch += [pltpu.SemaphoreType.DMA((d,))] * 8
    scratch += [pltpu.SemaphoreType.DMA((a,))] * 4
    scratch += [pltpu.SemaphoreType.DMA((d,))] * 4
    in_vmem = pl.BlockSpec(memory_space=pltpu.VMEM)
    in_smem = pl.BlockSpec(memory_space=pltpu.SMEM)
    return pl.pallas_call(
        kernel,
        out_shape=(jax.ShapeDtypeStruct(rows, F32), jax.ShapeDtypeStruct(rows, F32)),
        in_specs=[pl.BlockSpec(memory_space=pl.ANY), in_smem, in_smem, in_vmem, in_vmem, in_vmem],
        out_specs=(in_vmem, in_vmem),
        scratch_shapes=scratch,
        compiler_params=pltpu.CompilerParams(
            collective_id=0, has_side_effects=True, vmem_limit_bytes=60 * 1024 * 1024
        ),
        cost_estimate=pl.CostEstimate(flops=3_000_000_000, bytes_accessed=2_000_000, transcendentals=262144),
        name="gauss_newton",
    )(
        sensitivity.reshape(SLOTS, NY, 2, CENTRES, BLOCK), block_list.reshape(SLOTS), margin.T, centres,
        controls, observed,
    )


def solution(mesh):
    return jax.shard_map(
        local,
        mesh=mesh,
        in_specs=(
            P("stn", "cell", None, None, None),
            P("stn", "cell", None),
            P("cell", None),
            P("cell", None),
            P(("stn", "cell"), None),
            P(("stn", "cell"), None),
        ),
        out_specs=(P(("stn", "cell"), None), P(("stn", "cell"), None)),
        check_vma=False,
    )
```

```python
import jax
import jax.numpy as jnp
from jax import lax
from jax.experimental import pallas as pl
from jax.experimental.pallas import tpu as pltpu
from jax.sharding import PartitionSpec as P

MESH = pl.DeviceIdType.MESH
ITERS = 3
SLOTS, BLOCK, MARGINS, CENTRES, MEMBERS = 2, 512, 4, 32, 128
NX, NZ, NY = 4, 8, 8
NSTN, NCELL = NX * NZ, NY * 2
F32, BF16 = jnp.float32, jnp.bfloat16


def split(value):
    high = value.astype(BF16)
    low = (value - high.astype(F32)).astype(BF16)
    return high, low


def column_sum(value):
    return jnp.sum(value.reshape(-1, MEMBERS), axis=0, keepdims=True)


def interleave(first, second):
    upper = lax.broadcasted_iota(jnp.int32, first.shape, 1) < MARGINS
    even = jnp.where(upper, first, pltpu.roll(second, MARGINS, 1))
    odd = jnp.where(upper, pltpu.roll(first, MARGINS, 1), second)
    return even, odd


def kernel(
    sens_hbm, blocks, margin, centres, controls, observed, outputs,
    sens, sens_t, basis, basis_r, basis_t, coeff_rhs, cell_rhs, row_rhs, slope, pulled,
    list_in, hot, hot_t, same, entry_rhs,
    gath, part, core_in, paired, y_in, full, scat_out, scat_in, ans_out, ans_in,
    own_grad, own_dir, own_image, own_res, own_upd,
    row_core, row_core_in, row_y, row_y_in, row_s, row_s_in, row_c, row_c_in, pair_out, pair_in,
    sens_sem, li_s, li_r, gz_s, gz_r, gx_s, gx_r, hx_s, hx_r, hz_s, hz_r, cc_s, cc_r,
    c_s, c_r, y_s, y_r, fy_s, fy_r, fc_s, fc_r,
    sc_s, sc_r, an_s, an_r, rc_s, rc_r, ry_s, ry_r, rs_s, rs_r, pr_s, pr_r,
):
    stn, cell = lax.axis_index("stn"), lax.axis_index("cell")
    x, z = stn // NZ, stn % NZ
    y, core = cell // 2, cell % 2
    def ring(size, step):
        return min(step, size - step)

    far_y = sorted(range(1, NY), key=lambda d: -ring(NY, d))
    far_z = sorted(range(1, NZ), key=lambda d: -ring(NZ, d))
    far_x = sorted(range(1, NX), key=lambda d: -ring(NX, d))
    far_s = sorted(
        [(a, b) for a in range(NX) for b in range(NZ) if a or b],
        key=lambda d: -ring(NX, d[0]) - ring(NZ, d[1]),
    )
    x_peers = [((x + d) % NX, ((x + d) % NX) * NZ + z, cell) for d in far_x]
    z_peers = [((z + d) % NZ, x * NZ + (z + d) % NZ, cell) for d in far_z]
    y_peers = [((y + d) % NY, stn, ((y + d) % NY) * 2 + core) for d in far_y]
    y_others = [((y + d) % NY, stn, ((y + d) % NY) * 2 + 1 - core) for d in far_y]
    core_peer = (1 - core, stn, y * 2 + 1 - core)
    s_peers = [((x + a) % NX * NZ + (z + b) % NZ, (x + a) % NX * NZ + (z + b) % NZ, cell) for a, b in far_s]

    def send(src, dst, ssem, rsem, peer):
        pltpu.make_async_remote_copy(
            src_ref=src, dst_ref=dst, send_sem=ssem, recv_sem=rsem,
            device_id={"stn": peer[1], "cell": peer[2]}, device_id_type=MESH,
        ).start()

    def drain(ref, sem):
        pltpu.make_async_copy(ref, ref, sem).wait()

    barrier = pltpu.get_barrier_semaphore()
    everyone = z_peers + y_peers + x_peers + [core_peer]
    for peer in everyone:
        pl.semaphore_signal(
            barrier, inc=1, device_id={"stn": peer[1], "cell": peer[2]}, device_id_type=MESH
        )
    loads = [
        pltpu.make_async_copy(sens_hbm.at[n, :, side], sens.at[half, n], sens_sem.at[half * SLOTS + n])
        for half, side in ((0, 1 - core), (1, core)) for n in range(SLOTS)
    ]
    for load in loads:
        load.start()
    gath[x, z] = controls[...]
    pl.semaphore_wait(barrier, len(everyone))

    most, rest = pl.ds(0, 24), pl.ds(24, 8)
    for peer in z_peers:
        send(gath.at[x, z, most], gath.at[x, z, most], gz_s, gz_r, peer)
    for peer in x_peers:
        send(gath.at[x, z, rest], gath.at[x, z, rest], hx_s, hx_r, peer)

    listed = [[margin[o, blocks[n]] for o in range(MARGINS)] for n in range(SLOTS)]
    entry = lax.broadcasted_iota(jnp.int32, (SLOTS * MARGINS, MEMBERS), 0)
    lists = jnp.zeros((SLOTS * MARGINS, MEMBERS), F32)
    for n in range(SLOTS):
        for o in range(MARGINS):
            lists = jnp.where(entry == n * MARGINS + o, listed[n][o].astype(F32), lists)
    list_in[stn] = lists

    lane = lax.broadcasted_iota(jnp.int32, (8, MEMBERS), 1)
    rows_of_centres = [
        jnp.broadcast_to(centres[0:1, i * MEMBERS:(i + 1) * MEMBERS], (8, MEMBERS)) for i in range(8)
    ]
    to_row = lax.broadcasted_iota(jnp.int32, (MEMBERS, MEMBERS), 0)
    to_col = lax.broadcasted_iota(jnp.int32, (MEMBERS, MEMBERS), 1)
    by_row = (to_row == (to_col % MARGINS) * CENTRES + to_col // MARGINS).astype(BF16)
    for n in range(SLOTS):
        block = blocks[n]
        centre = jnp.zeros((8, MEMBERS), jnp.int32)
        for o in range(MARGINS):
            j = listed[n][o]
            row = rows_of_centres[0]
            for i in range(1, 8):
                row = jnp.where(j // 4 == i, rows_of_centres[i], row)
            turned = row
            for i in range(1, 4):
                turned = jnp.where((o + 4 - j % 4) % 4 == i, pltpu.roll(row, i * CENTRES, 1), turned)
            centre = jnp.where(lane // CENTRES == o, turned, centre)
        centre = centre[0:1]
        cells = lax.broadcasted_iota(jnp.int32, (BLOCK, MEMBERS), 0) + block * BLOCK
        squared = jnp.zeros((BLOCK, MEMBERS), F32)
        for shift, mask in ((10, 1048575), (5, 31), (0, 31)):
            cell_coord = ((cells >> shift) & mask).astype(F32)
            centre_coord = ((centre >> shift) & mask).astype(F32)
            spread = cell_coord - centre_coord
            squared = squared + spread * spread
        table = jnp.exp(squared * (-0.5 / 100.0))
        high, low = split(table)
        basis[n, :, 0:MEMBERS] = high
        basis[n, :, MEMBERS:] = low
        high = jnp.dot(high, by_row, preferred_element_type=F32)
        low = jnp.dot(low, by_row, preferred_element_type=F32)
        basis_r[n, :, 0:MEMBERS] = high.astype(BF16)
        basis_r[n, :, MEMBERS:] = low.astype(BF16)
        basis_t[n, 0:MEMBERS] = high.T.astype(BF16)
        basis_t[n, MEMBERS:] = low.T.astype(BF16)

    drain(gath.at[0, 0:NZ - 1, most], gz_r)
    for peer in x_peers:
        send(gath.at[x, :, most], gath.at[x, :, most], gx_s, gx_r, peer)
    drain(gath.at[0:NX - 1, 0, rest], hx_r)
    for peer in z_peers:
        send(gath.at[:, z, rest], gath.at[:, z, rest], hz_s, hz_r, peer)
    for load in loads:
        load.wait()
    for half in range(2):
        for n in range(SLOTS):
            for i in range(2):
                piece = sens[half, n, i * 4:(i + 1) * 4].reshape(128, BLOCK)
                sens_t[half, n * BLOCK:(n + 1) * BLOCK, i * 128:(i + 1) * 128] = piece.T
    drain(gath.at[0:NX - 1, :, most], gx_r)
    drain(gath.at[:, 0:NZ - 1, rest], hz_r)

    def send_lists():
        for peer in s_peers:
            send(list_in.at[stn], list_in.at[stn], li_s, li_r, peer)

    def use_lists():
        drain(list_in.at[0:NSTN - 1], li_r)
        flat_lists = list_in[...].reshape(NSTN * SLOTS * MARGINS, MEMBERS)
        found = (flat_lists == lax.broadcasted_iota(jnp.int32, flat_lists.shape, 1).astype(F32)).astype(F32)
        hot[...] = found.astype(BF16)
        found_t = found.T.astype(BF16)
        hot_t[...] = found_t[0:NSTN]
        same[...] = jnp.dot(hot[...], found_t, preferred_element_type=F32).astype(BF16)

    def times_basis(table, n):
        both = jnp.dot(table[n], coeff_rhs[n], preferred_element_type=F32)
        return both[:, 0:MEMBERS] + both[:, MEMBERS:]

    def put_coeffs(n, at, rows, value):
        high, low = split(value)
        for base in (0, MEMBERS):
            coeff_rhs[n, base + at:base + at + rows, 0:MEMBERS] = high
            coeff_rhs[n, base + at:base + at + rows, MEMBERS:] = low

    def both_ways(left, rhs):
        both = jnp.dot(left, rhs, preferred_element_type=F32)
        return both[:, 0:MEMBERS] + both[:, MEMBERS:]

    def station_rows(half):
        both = jnp.dot(sens[half, 0].reshape(BLOCK // 2, BLOCK), cell_rhs[0], preferred_element_type=F32)
        both += jnp.dot(sens[half, 1].reshape(BLOCK // 2, BLOCK), cell_rhs[1], preferred_element_type=F32)
        return (both[:, 0:MEMBERS] + both[:, MEMBERS:]).reshape(NY, CENTRES, MEMBERS)

    def put_cells(n, value):
        high, low = split(value)
        cell_rhs[n, :, 0:MEMBERS] = high
        cell_rhs[n, :, MEMBERS:] = low

    def share_row(i):
        drain(row_core_in.at[i], rc_r.at[i])
        row_y[i] = row_core[i] + row_core_in[i]
        for peer in y_peers:
            send(row_y.at[i], row_y_in.at[i, y], ry_s.at[i], ry_r.at[i], peer)
        row_y_in[i, y] = row_y[i]

    def shared_row(i):
        drain(row_y_in.at[i, 0:NY - 1], ry_r.at[i])
        return sum(row_y_in[i, j] for j in range(NY))

    def sum_cells(k, group_norm=None, meanwhile=None):
        part[k] = station_rows(0)
        send(part.at[k], core_in.at[k], c_s.at[k], c_r.at[k], core_peer)
        own_rows = station_rows(1)
        if group_norm is not None:
            row_core[k] = group_norm()
            send(row_core.at[k], row_core_in.at[k], rc_s.at[k], rc_r.at[k], core_peer)
        drain(core_in.at[k], c_r.at[k])
        paired[k] = own_rows + core_in[k]
        for peer in y_peers:
            send(paired.at[k, peer[0]], y_in.at[k, y], y_s.at[k], y_r.at[k], peer)
        y_in[k, y] = paired[k, y]
        if meanwhile is not None:
            meanwhile()
        norm = None
        if group_norm is not None:
            share_row(k)
            norm = shared_row(k)
        drain(y_in.at[k, 0:NY - 1], y_r.at[k])
        return sum(y_in[k, i] for i in range(NY)), norm

    def gather_cells(k, rows, with_curvature=True):
        full[k, 1, y] = rows
        for peer in y_peers:
            send(full.at[k, 1, y], full.at[k, 1, y], fy_s.at[k], fy_r.at[k], peer)
        if with_curvature:
            row_s[k] = column_sum(rows * rows)
            for peer in s_peers:
                send(row_s.at[k], row_s_in.at[k, stn], rs_s.at[k], rs_r.at[k], peer)
            row_s_in[k, stn] = row_s[k]

    def pull(half):
        return both_ways(sens_t[half], row_rhs[half]).reshape(SLOTS, BLOCK, MEMBERS)

    def put_rows(half, value):
        high, low = split(value)
        row_rhs[half, :, 0:MEMBERS] = high
        row_rhs[half, :, MEMBERS:] = low

    def adjoint(k, with_curvature):
        drain(full.at[k, 1, 0:NY - 1], fy_r.at[k])
        send(full.at[k, 1], full.at[k, 0], fc_s.at[k], fc_r.at[k], core_peer)
        put_rows(1, full[k, 1].reshape(BLOCK // 2, MEMBERS))
        pulled[...] = pull(1)
        if with_curvature:
            drain(row_s_in.at[k, 0:NSTN - 1], rs_r.at[k])
            row_core[ITERS + k] = sum(row_s_in[k, i] for i in range(NSTN))
            send(row_core.at[ITERS + k], row_core_in.at[ITERS + k], rc_s.at[ITERS + k], rc_r.at[ITERS + k], core_peer)
        drain(full.at[k, 0], fc_r.at[k])
        put_rows(0, full[k, 0].reshape(BLOCK // 2, MEMBERS))
        rest_of = pull(0)
        for n in range(SLOTS):
            put_cells(n, slope[n] * (pulled[n] + rest_of[n]))
        if with_curvature:
            share_row(ITERS + k)
        parts = []
        for n in range(SLOTS):
            two = both_ways(basis_t[n], cell_rhs[n])
            parts.append((two[0:MEMBERS] + two[MEMBERS:]).reshape(CENTRES // 2, 2 * MARGINS, MEMBERS))
        even, odd = interleave(parts[0], parts[1])
        scat_out[k, :, 0] = even
        scat_out[k, :, 1] = odd
        for peer in s_peers:
            send(scat_out.at[k, peer[0] // 2, peer[0] % 2], scat_in.at[k, stn], sc_s.at[k], sc_r.at[k], peer)
        scat_in[k, stn] = scat_out[k, stn // 2, stn % 2]
        curvature = None
        if with_curvature:
            curvature = shared_row(ITERS + k)
        drain(scat_in.at[k, 0:NSTN - 1], sc_r.at[k])
        high, low = split(scat_in[k].reshape(NSTN * SLOTS * MARGINS, MEMBERS))
        entry_rhs[:, 0:MEMBERS] = high
        entry_rhs[:, MEMBERS:] = low
        return curvature

    def own_change():
        return both_ways(hot_t[...], entry_rhs[...])

    def answer(k, step=None):
        change = both_ways(same[...], entry_rhs[...]).reshape(NSTN, SLOTS * MARGINS, MEMBERS)
        ans_out[k] = change if step is None else ans_out[k - 1] - step * change
        for peer in s_peers:
            send(ans_out.at[k, peer[0]], ans_in.at[k, stn], an_s.at[k], an_r.at[k], peer)
        ans_in[k, stn] = ans_out[k, stn]
        own = own_change() if step is None else own_grad[...] - step * own_change()
        own_grad[...] = own
        square = column_sum(own * own)
        for j in range(NSTN):
            pair_out[k, j, 0:1] = own[j:j + 1]
            pair_out[k, j, 1:2] = square
        for peer in s_peers:
            send(pair_out.at[k, peer[0]], pair_in.at[k, stn], pr_s.at[k], pr_r.at[k], peer)
        pair_in[k, stn] = pair_out[k, stn]

    for n in range(SLOTS):
        for o in range(MARGINS):
            put_coeffs(n, o * CENTRES, CENTRES, gath[listed[n][o] // NZ, listed[n][o] % NZ])
        tanh_phi = jnp.tanh(times_basis(basis, n))
        slope[n] = 0.5 * (1.0 - tanh_phi * tanh_phi)
        put_cells(n, 0.5 * (1.0 + tanh_phi))
    predicted, _ = sum_cells(0, meanwhile=send_lists)
    own_res[...] = observed[...] - predicted
    gather_cells(0, own_res[...], False)
    use_lists()
    adjoint(0, False)
    answer(0)

    norm = None
    for k in range(1, ITERS + 1):
        drain(ans_in.at[k - 1, 0:NSTN - 1], an_r.at[k - 1])
        tiles = ans_in[k - 1].reshape(CENTRES // 2, 2, SLOTS * MARGINS, MEMBERS)
        for n, tile in enumerate(interleave(tiles[:, 0], tiles[:, 1])):
            put_coeffs(n, 0, MEMBERS, tile.reshape(MEMBERS, MEMBERS))
        fields = [times_basis(basis_r, n) for n in range(SLOTS)]
        for n in range(SLOTS):
            put_cells(n, slope[n] * fields[n])

        def group_norm():
            drain(pair_in.at[k - 1, 0:NSTN - 1], pr_r.at[k - 1])
            return sum(pair_in[k - 1, i, 1:2] for i in range(NSTN))

        image, new_norm = sum_cells(k, group_norm)
        ratio = new_norm / norm if k > 1 else None
        if k > 1:
            image = image + ratio * own_image[...]
        norm = new_norm
        own_image[...] = image
        if k < ITERS:
            gather_cells(k, image)
        else:
            row_c[...] = column_sum(image * image)
            for peer in y_others + y_peers + [core_peer]:
                send(row_c, row_c_in.at[cell], cc_s, cc_r, peer)
        direction = jnp.concatenate([pair_in[k - 1, i, 0:1] for i in range(NSTN)], axis=0)
        if k > 1:
            direction = direction + ratio * own_dir[...]
        own_dir[...] = direction
        if k < ITERS:
            curvature = adjoint(k, True)
            step = norm / curvature
            answer(k, step)
        else:
            row_c_in[cell] = row_c[...]
            drain(row_c_in.at[0:NCELL - 1], cc_r)
            row_s[0] = sum(row_c_in[i] for i in range(NCELL))
            for peer in s_peers:
                send(row_s.at[0], row_s_in.at[0, stn], rs_s.at[0], rs_r.at[0], peer)
            row_s_in[0, stn] = row_s[0]
            drain(row_s_in.at[0, 0:NSTN - 1], rs_r.at[0])
            step = norm / sum(row_s_in[0, i] for i in range(NSTN))
        own_res[...] = own_res[...] - step * image
        own_upd[...] = step * direction if k == 1 else own_upd[...] + step * direction

    outputs[0:CENTRES] = controls[...] + own_upd[...]
    outputs[CENTRES:] = own_res[...]

    drain(gath.at[0, 0:NZ - 1, most], gz_s)
    drain(gath.at[0:NX - 1, :, most], gx_s)
    drain(gath.at[0:NX - 1, 0, rest], hx_s)
    drain(gath.at[:, 0:NZ - 1, rest], hz_s)
    drain(row_c_in.at[0:NCELL - 1], cc_s)
    drain(list_in.at[0:NSTN - 1], li_s)
    for k in range(ITERS + 1):
        drain(core_in.at[k], c_s.at[k])
        drain(y_in.at[k, 0:NY - 1], y_s.at[k])
    for k in range(1, 2 * ITERS):
        drain(row_core_in.at[k], rc_s.at[k])
        drain(row_y_in.at[k, 0:NY - 1], ry_s.at[k])
    for k in range(ITERS):
        drain(full.at[k, 1, 0:NY - 1], fy_s.at[k])
        drain(full.at[k, 1], fc_s.at[k])
        drain(scat_in.at[k, 0:NSTN - 1], sc_s.at[k])
        drain(ans_in.at[k, 0:NSTN - 1], an_s.at[k])
        drain(row_s_in.at[k, 0:NSTN - 1], rs_s.at[k])
        drain(pair_in.at[k, 0:NSTN - 1], pr_s.at[k])


def local(sensitivity, block_list, margin, centres, controls, observed):
    rows = (CENTRES, MEMBERS)
    a, d, r = ITERS + 1, ITERS, 2 * ITERS

    def vmem(*shape):
        return pltpu.VMEM(shape, F32)

    entries = SLOTS * MARGINS
    scratch = [
        pltpu.VMEM((2, SLOTS, NY, CENTRES, BLOCK), BF16),
        pltpu.VMEM((2, SLOTS * BLOCK, BLOCK // 2), BF16),
        pltpu.VMEM((SLOTS, BLOCK, 2 * MEMBERS), BF16),
        pltpu.VMEM((SLOTS, BLOCK, 2 * MEMBERS), BF16),
        pltpu.VMEM((SLOTS, 2 * MEMBERS, BLOCK), BF16),
        pltpu.VMEM((SLOTS, 2 * MEMBERS, 2 * MEMBERS), BF16),
        pltpu.VMEM((SLOTS, BLOCK, 2 * MEMBERS), BF16),
        pltpu.VMEM((2, BLOCK // 2, 2 * MEMBERS), BF16),
        vmem(SLOTS, BLOCK, MEMBERS),
        vmem(SLOTS, BLOCK, MEMBERS),
        vmem(NSTN, entries, MEMBERS),
        pltpu.VMEM((NSTN * entries, MEMBERS), BF16),
        pltpu.VMEM((NSTN, NSTN * entries), BF16),
        pltpu.VMEM((NSTN * entries, NSTN * entries), BF16),
        pltpu.VMEM((NSTN * entries, 2 * MEMBERS), BF16),
        vmem(NX, NZ, *rows),
        vmem(a, NY, *rows),
        vmem(a, NY, *rows),
        vmem(a, NY, *rows),
        vmem(a, NY, *rows),
        vmem(d, 2, NY, *rows),
        vmem(d, CENTRES // 2, 2, entries, MEMBERS),
        vmem(d, NSTN, entries, MEMBERS),
        vmem(d, NSTN, entries, MEMBERS),
        vmem(d, NSTN, entries, MEMBERS),
        vmem(*rows), vmem(*rows), vmem(*rows), vmem(*rows), vmem(*rows),
        vmem(r, 1, MEMBERS), vmem(r, 1, MEMBERS),
        vmem(r, 1, MEMBERS), vmem(r, NY, 1, MEMBERS),
        vmem(d, 1, MEMBERS), vmem(d, NSTN, 1, MEMBERS),
        vmem(1, MEMBERS), vmem(NCELL, 1, MEMBERS),
        vmem(d, NSTN, 2, MEMBERS), vmem(d, NSTN, 2, MEMBERS),
    ]
    scratch += [pltpu.SemaphoreType.DMA((2 * SLOTS,))]
    scratch += [pltpu.SemaphoreType.DMA] * 12
    scratch += [pltpu.SemaphoreType.DMA((a,))] * 4
    scratch += [pltpu.SemaphoreType.DMA((d,))] * 8
    scratch += [pltpu.SemaphoreType.DMA((r,))] * 4
    scratch += [pltpu.SemaphoreType.DMA((d,))] * 4
    in_vmem = pl.BlockSpec(memory_space=pltpu.VMEM)
    in_smem = pl.BlockSpec(memory_space=pltpu.SMEM)
    outputs = pl.pallas_call(
        kernel,
        out_shape=jax.ShapeDtypeStruct((2 * CENTRES, MEMBERS), F32),
        in_specs=[pl.BlockSpec(memory_space=pl.ANY), in_smem, in_smem, in_vmem, in_vmem, in_vmem],
        out_specs=in_vmem,
        scratch_shapes=scratch,
        compiler_params=pltpu.CompilerParams(
            collective_id=0, has_side_effects=True, vmem_limit_bytes=60 * 1024 * 1024
        ),
        cost_estimate=pl.CostEstimate(flops=3_000_000_000, bytes_accessed=2_000_000, transcendentals=262144),
        name="gauss_newton",
    )(
        sensitivity.reshape(SLOTS, NY, 2, CENTRES, BLOCK), block_list.reshape(SLOTS), margin.T, centres,
        controls, observed,
    )
    return outputs[:CENTRES], outputs[CENTRES:]


def solution(mesh):
    return jax.shard_map(
        local,
        mesh=mesh,
        in_specs=(
            P("stn", "cell", None, None, None),
            P("stn", "cell", None),
            P("cell", None),
            P("cell", None),
            P(("stn", "cell"), None),
            P(("stn", "cell"), None),
        ),
        out_specs=(P(("stn", "cell"), None), P(("stn", "cell"), None)),
        check_vma=False,
    )
```

```python
import jax
import jax.numpy as jnp
from jax import lax
from jax.experimental import pallas as pl
from jax.experimental.pallas import tpu as pltpu
from jax.sharding import PartitionSpec as P

MESH = pl.DeviceIdType.MESH
ITERS = 3
SLOTS, BLOCK, MARGINS, CENTRES, MEMBERS = 2, 512, 4, 32, 128
NX, NZ, NY = 4, 8, 8
NSTN, NCELL = NX * NZ, NY * 2
F32, BF16 = jnp.float32, jnp.bfloat16


def split(value):
    high = value.astype(BF16)
    low = (value - high.astype(F32)).astype(BF16)
    return high, low


def column_sum(value):
    return jnp.sum(value.reshape(-1, MEMBERS), axis=0, keepdims=True)


def interleave(first, second):
    upper = lax.broadcasted_iota(jnp.int32, first.shape, 1) < MARGINS
    even = jnp.where(upper, first, pltpu.roll(second, MARGINS, 1))
    odd = jnp.where(upper, pltpu.roll(first, MARGINS, 1), second)
    return even, odd


def kernel(
    sens_hbm, blocks_hbm, margin_hbm, centres_hbm, controls, observed_hbm, outputs,
    blocks, margin, centres, observed, sens, sens_t, basis, basis_r, basis_t, coeff_rhs, cell_rhs, row_rhs, slope, pulled,
    list_in, hot, hot_t, same, entry_rhs,
    gath, part, core_in, paired, y_in, full, scat_out, scat_in, ans_out, ans_in,
    own_grad, own_dir, own_image, own_res, own_upd,
    row_core, row_core_in, row_y, row_y_in, row_s, row_s_in, row_c, row_c_in, pair_out, pair_in,
    sens_sem, blocks_sem, margin_sem, centres_sem, controls_sem, observed_sem, li_s, li_r, gz_s, gz_r, gx_s, gx_r, hx_s, hx_r, hz_s, hz_r, cc_s, cc_r,
    c_s, c_r, y_s, y_r, fy_s, fy_r, fc_s, fc_r,
    sc_s, sc_r, an_s, an_r, rc_s, rc_r, ry_s, ry_r, rs_s, rs_r, pr_s, pr_r,
):
    stn, cell = lax.axis_index("stn"), lax.axis_index("cell")
    x, z = stn // NZ, stn % NZ
    y, core = cell // 2, cell % 2
    def ring(size, step):
        return min(step, size - step)

    far_y = sorted(range(1, NY), key=lambda d: -ring(NY, d))
    far_z = sorted(range(1, NZ), key=lambda d: -ring(NZ, d))
    far_x = sorted(range(1, NX), key=lambda d: -ring(NX, d))
    far_s = sorted(
        [(a, b) for a in range(NX) for b in range(NZ) if a or b],
        key=lambda d: -ring(NX, d[0]) - ring(NZ, d[1]),
    )
    x_peers = [((x + d) % NX, ((x + d) % NX) * NZ + z, cell) for d in far_x]
    z_peers = [((z + d) % NZ, x * NZ + (z + d) % NZ, cell) for d in far_z]
    y_peers = [((y + d) % NY, stn, ((y + d) % NY) * 2 + core) for d in far_y]
    y_others = [((y + d) % NY, stn, ((y + d) % NY) * 2 + 1 - core) for d in far_y]
    core_peer = (1 - core, stn, y * 2 + 1 - core)
    s_peers = [((x + a) % NX * NZ + (z + b) % NZ, (x + a) % NX * NZ + (z + b) % NZ, cell) for a, b in far_s]

    def send(src, dst, ssem, rsem, peer):
        pltpu.make_async_remote_copy(
            src_ref=src, dst_ref=dst, send_sem=ssem, recv_sem=rsem,
            device_id={"stn": peer[1], "cell": peer[2]}, device_id_type=MESH,
        ).start()

    def drain(ref, sem):
        pltpu.make_async_copy(ref, ref, sem).wait()

    barrier = pltpu.get_barrier_semaphore()
    everyone = z_peers + y_peers + x_peers + [core_peer]
    for peer in everyone:
        pl.semaphore_signal(
            barrier, inc=1, device_id={"stn": peer[1], "cell": peer[2]}, device_id_type=MESH
        )
    first = pltpu.make_async_copy(controls, gath.at[x, z], controls_sem)
    first.start()
    small = [
        pltpu.make_async_copy(src, dst, sem) for src, dst, sem in (
            (blocks_hbm, blocks, blocks_sem), (margin_hbm, margin, margin_sem),
            (centres_hbm, centres, centres_sem), (observed_hbm, observed, observed_sem),
        )
    ]
    for copy in small:
        copy.start()
    for half, side in ((0, 1 - core), (1, core)):
        for n in range(SLOTS):
            for p, d in enumerate(far_y + [0]):
                pltpu.make_async_copy(
                    sens_hbm.at[n, (y + d) % NY, side], sens.at[half, n, p], sens_sem.at[half * SLOTS + n]
                ).start()
    first.wait()
    pl.semaphore_wait(barrier, len(everyone))

    most, rest = pl.ds(0, 24), pl.ds(24, 8)
    for peer in z_peers:
        send(gath.at[x, z, most], gath.at[x, z, most], gz_s, gz_r, peer)
    for peer in x_peers:
        send(gath.at[x, z, rest], gath.at[x, z, rest], hx_s, hx_r, peer)

    for copy in small:
        copy.wait()
    listed = [[margin[o, blocks[0, n]] for o in range(MARGINS)] for n in range(SLOTS)]
    entry = lax.broadcasted_iota(jnp.int32, (SLOTS * MARGINS, MEMBERS), 0)
    lists = jnp.zeros((SLOTS * MARGINS, MEMBERS), F32)
    for n in range(SLOTS):
        for o in range(MARGINS):
            lists = jnp.where(entry == n * MARGINS + o, listed[n][o].astype(F32), lists)
    list_in[stn] = lists

    lane = lax.broadcasted_iota(jnp.int32, (8, MEMBERS), 1)
    rows_of_centres = [
        jnp.broadcast_to(centres[0:1, i * MEMBERS:(i + 1) * MEMBERS], (8, MEMBERS)) for i in range(8)
    ]
    to_row = lax.broadcasted_iota(jnp.int32, (MEMBERS, MEMBERS), 0)
    to_col = lax.broadcasted_iota(jnp.int32, (MEMBERS, MEMBERS), 1)
    by_row = (to_row == (to_col % MARGINS) * CENTRES + to_col // MARGINS).astype(BF16)
    for n in range(SLOTS):
        block = blocks[0, n]
        centre = jnp.zeros((8, MEMBERS), jnp.int32)
        for o in range(MARGINS):
            j = listed[n][o]
            row = rows_of_centres[0]
            for i in range(1, 8):
                row = jnp.where(j // 4 == i, rows_of_centres[i], row)
            turned = row
            for i in range(1, 4):
                turned = jnp.where((o + 4 - j % 4) % 4 == i, pltpu.roll(row, i * CENTRES, 1), turned)
            centre = jnp.where(lane // CENTRES == o, turned, centre)
        centre = centre[0:1]
        cells = lax.broadcasted_iota(jnp.int32, (BLOCK, MEMBERS), 0) + block * BLOCK
        squared = jnp.zeros((BLOCK, MEMBERS), F32)
        for shift, mask in ((10, 1048575), (5, 31), (0, 31)):
            cell_coord = ((cells >> shift) & mask).astype(F32)
            centre_coord = ((centre >> shift) & mask).astype(F32)
            spread = cell_coord - centre_coord
            squared = squared + spread * spread
        table = jnp.exp(squared * (-0.5 / 100.0))
        high, low = split(table)
        basis[n, :, 0:MEMBERS] = high
        basis[n, :, MEMBERS:] = low
        high = jnp.dot(high, by_row, preferred_element_type=F32)
        low = jnp.dot(low, by_row, preferred_element_type=F32)
        basis_r[n, :, 0:MEMBERS] = high.astype(BF16)
        basis_r[n, :, MEMBERS:] = low.astype(BF16)
        basis_t[n, 0:MEMBERS] = high.T.astype(BF16)
        basis_t[n, MEMBERS:] = low.T.astype(BF16)

    drain(gath.at[0, 0:NZ - 1, most], gz_r)
    for peer in x_peers:
        send(gath.at[x, :, most], gath.at[x, :, most], gx_s, gx_r, peer)
    drain(gath.at[0:NX - 1, 0, rest], hx_r)
    for peer in z_peers:
        send(gath.at[:, z, rest], gath.at[:, z, rest], hz_s, hz_r, peer)
    for half in range(2):
        for n in range(SLOTS):
            drain(sens.at[half, n], sens_sem.at[half * SLOTS + n])
            for i in range(2):
                piece = sens[half, n, i * 4:(i + 1) * 4].reshape(128, BLOCK)
                sens_t[half, n * BLOCK:(n + 1) * BLOCK, i * 128:(i + 1) * 128] = piece.T
    drain(gath.at[0:NX - 1, :, most], gx_r)
    drain(gath.at[:, 0:NZ - 1, rest], hz_r)

    def send_lists():
        for peer in s_peers:
            send(list_in.at[stn], list_in.at[stn], li_s, li_r, peer)

    def use_lists():
        drain(list_in.at[0:NSTN - 1], li_r)
        flat_lists = list_in[...].reshape(NSTN * SLOTS * MARGINS, MEMBERS)
        found = (flat_lists == lax.broadcasted_iota(jnp.int32, flat_lists.shape, 1).astype(F32)).astype(F32)
        hot[...] = found.astype(BF16)
        found_t = found.T.astype(BF16)
        hot_t[...] = found_t[0:NSTN]
        same[...] = jnp.dot(hot[...], found_t, preferred_element_type=F32).astype(BF16)

    def times_basis(table, n):
        both = jnp.dot(table[n], coeff_rhs[n], preferred_element_type=F32)
        return both[:, 0:MEMBERS] + both[:, MEMBERS:]

    def put_coeffs(n, at, rows, value):
        high, low = split(value)
        for base in (0, MEMBERS):
            coeff_rhs[n, base + at:base + at + rows, 0:MEMBERS] = high
            coeff_rhs[n, base + at:base + at + rows, MEMBERS:] = low

    def both_ways(left, rhs):
        both = jnp.dot(left, rhs, preferred_element_type=F32)
        return both[:, 0:MEMBERS] + both[:, MEMBERS:]

    def station_rows(half):
        both = jnp.dot(sens[half, 0].reshape(BLOCK // 2, BLOCK), cell_rhs[0], preferred_element_type=F32)
        both += jnp.dot(sens[half, 1].reshape(BLOCK // 2, BLOCK), cell_rhs[1], preferred_element_type=F32)
        return (both[:, 0:MEMBERS] + both[:, MEMBERS:]).reshape(NY, CENTRES, MEMBERS)

    def put_cells(n, value):
        high, low = split(value)
        cell_rhs[n, :, 0:MEMBERS] = high
        cell_rhs[n, :, MEMBERS:] = low

    def share_row(i):
        drain(row_core_in.at[i], rc_r.at[i])
        row_y[i] = row_core[i] + row_core_in[i]
        for peer in y_peers:
            send(row_y.at[i], row_y_in.at[i, y], ry_s.at[i], ry_r.at[i], peer)
        row_y_in[i, y] = row_y[i]

    def shared_row(i):
        drain(row_y_in.at[i, 0:NY - 1], ry_r.at[i])
        return sum(row_y_in[i, j] for j in range(NY))

    groups = (slice(0, 3), slice(3, NY))
    place = {d: p for p, d in enumerate(far_y + [0])}

    def sum_cells(k, group_norm=None, meanwhile=None):
        part[k] = station_rows(0)
        for g, blocks_of in enumerate(groups):
            send(part.at[k, blocks_of], core_in.at[k, blocks_of], c_s.at[2 * k + g], c_r.at[2 * k + g], core_peer)
        own_rows = station_rows(1)
        if group_norm is not None:
            row_core[k] = group_norm()
            send(row_core.at[k], row_core_in.at[k], rc_s.at[k], rc_r.at[k], core_peer)
        for g, blocks_of in enumerate(groups):
            drain(core_in.at[k, blocks_of], c_r.at[2 * k + g])
            paired[k, blocks_of] = own_rows[blocks_of] + core_in[k, blocks_of]
            for p, peer in list(enumerate(y_peers))[blocks_of]:
                send(paired.at[k, p], y_in.at[k, y], y_s.at[k], y_r.at[k], peer)
        y_in[k, y] = paired[k, NY - 1]
        if meanwhile is not None:
            meanwhile()
        norm = None
        if group_norm is not None:
            share_row(k)
            norm = shared_row(k)
        drain(y_in.at[k, 0:NY - 1], y_r.at[k])
        return sum(y_in[k, i] for i in range(NY)), norm

    def gather_cells(k, rows, with_curvature=True):
        full[k, 1, NY - 1] = rows
        for p, peer in enumerate(y_peers):
            g = int(p >= 3)
            send(
                full.at[k, 1, NY - 1], full.at[k, 1, place[NY - far_y[p]]],
                fy_s.at[2 * k + g], fy_r.at[2 * k + g], peer,
            )
        if with_curvature:
            row_s[k] = column_sum(rows * rows)
            for peer in s_peers:
                send(row_s.at[k], row_s_in.at[k, stn], rs_s.at[k], rs_r.at[k], peer)
            row_s_in[k, stn] = row_s[k]

    def pull(half):
        return both_ways(sens_t[half], row_rhs[half]).reshape(SLOTS, BLOCK, MEMBERS)

    def put_rows(half, value):
        high, low = split(value)
        row_rhs[half, :, 0:MEMBERS] = high
        row_rhs[half, :, MEMBERS:] = low

    def adjoint(k, with_curvature):
        for g, arrived in ((1, slice(3, NY - 1)), (0, slice(0, 3))):
            drain(full.at[k, 1, arrived], fy_r.at[2 * k + g])
            send(
                full.at[k, 1, groups[g]], full.at[k, 0, groups[g]],
                fc_s.at[2 * k + g], fc_r.at[2 * k + g], core_peer,
            )
        put_rows(1, full[k, 1].reshape(BLOCK // 2, MEMBERS))
        pulled[...] = pull(1)
        if with_curvature:
            drain(row_s_in.at[k, 0:NSTN - 1], rs_r.at[k])
            row_core[ITERS + k] = sum(row_s_in[k, i] for i in range(NSTN))
            send(row_core.at[ITERS + k], row_core_in.at[ITERS + k], rc_s.at[ITERS + k], rc_r.at[ITERS + k], core_peer)
        for g in (1, 0):
            drain(full.at[k, 0, groups[g]], fc_r.at[2 * k + g])
        put_rows(0, full[k, 0].reshape(BLOCK // 2, MEMBERS))
        rest_of = pull(0)
        for n in range(SLOTS):
            put_cells(n, slope[n] * (pulled[n] + rest_of[n]))
        if with_curvature:
            share_row(ITERS + k)
        parts = []
        for n in range(SLOTS):
            two = both_ways(basis_t[n], cell_rhs[n])
            parts.append((two[0:MEMBERS] + two[MEMBERS:]).reshape(CENTRES // 2, 2 * MARGINS, MEMBERS))
        even, odd = interleave(parts[0], parts[1])
        scat_out[k, :, 0] = even
        scat_out[k, :, 1] = odd
        for peer in s_peers:
            send(scat_out.at[k, peer[0] // 2, peer[0] % 2], scat_in.at[k, stn], sc_s.at[k], sc_r.at[k], peer)
        scat_in[k, stn] = scat_out[k, stn // 2, stn % 2]
        curvature = None
        if with_curvature:
            curvature = shared_row(ITERS + k)
        drain(scat_in.at[k, 0:NSTN - 1], sc_r.at[k])
        high, low = split(scat_in[k].reshape(NSTN * SLOTS * MARGINS, MEMBERS))
        entry_rhs[:, 0:MEMBERS] = high
        entry_rhs[:, MEMBERS:] = low
        return curvature

    def own_change():
        return both_ways(hot_t[...], entry_rhs[...])

    def answer(k, step=None):
        change = both_ways(same[...], entry_rhs[...]).reshape(NSTN, SLOTS * MARGINS, MEMBERS)
        ans_out[k] = change if step is None else ans_out[k - 1] - step * change
        for peer in s_peers:
            send(ans_out.at[k, peer[0]], ans_in.at[k, stn], an_s.at[k], an_r.at[k], peer)
        ans_in[k, stn] = ans_out[k, stn]
        own = own_change() if step is None else own_grad[...] - step * own_change()
        own_grad[...] = own
        square = column_sum(own * own)
        for j in range(NSTN):
            pair_out[k, j, 0:1] = own[j:j + 1]
            pair_out[k, j, 1:2] = square
        for peer in s_peers:
            send(pair_out.at[k, peer[0]], pair_in.at[k, stn], pr_s.at[k], pr_r.at[k], peer)
        pair_in[k, stn] = pair_out[k, stn]

    for n in range(SLOTS):
        for o in range(MARGINS):
            put_coeffs(n, o * CENTRES, CENTRES, gath[listed[n][o] // NZ, listed[n][o] % NZ])
        tanh_phi = jnp.tanh(times_basis(basis, n))
        slope[n] = 0.5 * (1.0 - tanh_phi * tanh_phi)
        put_cells(n, 0.5 * (1.0 + tanh_phi))
    predicted, _ = sum_cells(0, meanwhile=send_lists)
    own_res[...] = observed[...] - predicted
    gather_cells(0, own_res[...], False)
    use_lists()
    adjoint(0, False)
    answer(0)

    norm = None
    for k in range(1, ITERS + 1):
        drain(ans_in.at[k - 1, 0:NSTN - 1], an_r.at[k - 1])
        tiles = ans_in[k - 1].reshape(CENTRES // 2, 2, SLOTS * MARGINS, MEMBERS)
        for n, tile in enumerate(interleave(tiles[:, 0], tiles[:, 1])):
            put_coeffs(n, 0, MEMBERS, tile.reshape(MEMBERS, MEMBERS))
        fields = [times_basis(basis_r, n) for n in range(SLOTS)]
        for n in range(SLOTS):
            put_cells(n, slope[n] * fields[n])

        def group_norm():
            drain(pair_in.at[k - 1, 0:NSTN - 1], pr_r.at[k - 1])
            return sum(pair_in[k - 1, i, 1:2] for i in range(NSTN))

        image, new_norm = sum_cells(k, group_norm)
        ratio = new_norm / norm if k > 1 else None
        if k > 1:
            image = image + ratio * own_image[...]
        norm = new_norm
        own_image[...] = image
        if k < ITERS:
            gather_cells(k, image)
        else:
            row_c[...] = column_sum(image * image)
            for peer in y_others + y_peers + [core_peer]:
                send(row_c, row_c_in.at[cell], cc_s, cc_r, peer)
        direction = jnp.concatenate([pair_in[k - 1, i, 0:1] for i in range(NSTN)], axis=0)
        if k > 1:
            direction = direction + ratio * own_dir[...]
        own_dir[...] = direction
        if k < ITERS:
            curvature = adjoint(k, True)
            step = norm / curvature
            answer(k, step)
        else:
            row_c_in[cell] = row_c[...]
            drain(row_c_in.at[0:NCELL - 1], cc_r)
            row_s[0] = sum(row_c_in[i] for i in range(NCELL))
            for peer in s_peers:
                send(row_s.at[0], row_s_in.at[0, stn], rs_s.at[0], rs_r.at[0], peer)
            row_s_in[0, stn] = row_s[0]
            drain(row_s_in.at[0, 0:NSTN - 1], rs_r.at[0])
            step = norm / sum(row_s_in[0, i] for i in range(NSTN))
        own_res[...] = own_res[...] - step * image
        own_upd[...] = step * direction if k == 1 else own_upd[...] + step * direction

    outputs[0:CENTRES] = gath[x, z] + own_upd[...]
    outputs[CENTRES:] = own_res[...]

    drain(gath.at[0, 0:NZ - 1, most], gz_s)
    drain(gath.at[0:NX - 1, :, most], gx_s)
    drain(gath.at[0:NX - 1, 0, rest], hx_s)
    drain(gath.at[:, 0:NZ - 1, rest], hz_s)
    drain(row_c_in.at[0:NCELL - 1], cc_s)
    drain(list_in.at[0:NSTN - 1], li_s)
    for k in range(ITERS + 1):
        for g in range(2):
            drain(core_in.at[k, groups[g]], c_s.at[2 * k + g])
        drain(y_in.at[k, 0:NY - 1], y_s.at[k])
    for k in range(1, 2 * ITERS):
        drain(row_core_in.at[k], rc_s.at[k])
        drain(row_y_in.at[k, 0:NY - 1], ry_s.at[k])
    for k in range(ITERS):
        for g, arrived in ((1, slice(3, NY - 1)), (0, slice(0, 3))):
            drain(full.at[k, 1, arrived], fy_s.at[2 * k + g])
            drain(full.at[k, 0, groups[g]], fc_s.at[2 * k + g])
        drain(scat_in.at[k, 0:NSTN - 1], sc_s.at[k])
        drain(ans_in.at[k, 0:NSTN - 1], an_s.at[k])
        drain(row_s_in.at[k, 0:NSTN - 1], rs_s.at[k])
        drain(pair_in.at[k, 0:NSTN - 1], pr_s.at[k])


def local(sensitivity, block_list, margin, centres, controls, observed):
    rows = (CENTRES, MEMBERS)
    a, d, r = ITERS + 1, ITERS, 2 * ITERS

    def vmem(*shape):
        return pltpu.VMEM(shape, F32)

    entries = SLOTS * MARGINS
    scratch = [
        pltpu.SMEM((1, SLOTS), jnp.int32),
        pltpu.SMEM((MARGINS, margin.shape[0]), jnp.int32),
        pltpu.VMEM(centres.shape, jnp.int32),
        vmem(*rows),
        pltpu.VMEM((2, SLOTS, NY, CENTRES, BLOCK), BF16),
        pltpu.VMEM((2, SLOTS * BLOCK, BLOCK // 2), BF16),
        pltpu.VMEM((SLOTS, BLOCK, 2 * MEMBERS), BF16),
        pltpu.VMEM((SLOTS, BLOCK, 2 * MEMBERS), BF16),
        pltpu.VMEM((SLOTS, 2 * MEMBERS, BLOCK), BF16),
        pltpu.VMEM((SLOTS, 2 * MEMBERS, 2 * MEMBERS), BF16),
        pltpu.VMEM((SLOTS, BLOCK, 2 * MEMBERS), BF16),
        pltpu.VMEM((2, BLOCK // 2, 2 * MEMBERS), BF16),
        vmem(SLOTS, BLOCK, MEMBERS),
        vmem(SLOTS, BLOCK, MEMBERS),
        vmem(NSTN, entries, MEMBERS),
        pltpu.VMEM((NSTN * entries, MEMBERS), BF16),
        pltpu.VMEM((NSTN, NSTN * entries), BF16),
        pltpu.VMEM((NSTN * entries, NSTN * entries), BF16),
        pltpu.VMEM((NSTN * entries, 2 * MEMBERS), BF16),
        vmem(NX, NZ, *rows),
        vmem(a, NY, *rows),
        vmem(a, NY, *rows),
        vmem(a, NY, *rows),
        vmem(a, NY, *rows),
        vmem(d, 2, NY, *rows),
        vmem(d, CENTRES // 2, 2, entries, MEMBERS),
        vmem(d, NSTN, entries, MEMBERS),
        vmem(d, NSTN, entries, MEMBERS),
        vmem(d, NSTN, entries, MEMBERS),
        vmem(*rows), vmem(*rows), vmem(*rows), vmem(*rows), vmem(*rows),
        vmem(r, 1, MEMBERS), vmem(r, 1, MEMBERS),
        vmem(r, 1, MEMBERS), vmem(r, NY, 1, MEMBERS),
        vmem(d, 1, MEMBERS), vmem(d, NSTN, 1, MEMBERS),
        vmem(1, MEMBERS), vmem(NCELL, 1, MEMBERS),
        vmem(d, NSTN, 2, MEMBERS), vmem(d, NSTN, 2, MEMBERS),
    ]
    scratch += [pltpu.SemaphoreType.DMA((2 * SLOTS,))]
    scratch += [pltpu.SemaphoreType.DMA] * 17
    scratch += [pltpu.SemaphoreType.DMA((2 * a,))] * 2
    scratch += [pltpu.SemaphoreType.DMA((a,))] * 2
    scratch += [pltpu.SemaphoreType.DMA((2 * d,))] * 4
    scratch += [pltpu.SemaphoreType.DMA((d,))] * 4
    scratch += [pltpu.SemaphoreType.DMA((r,))] * 4
    scratch += [pltpu.SemaphoreType.DMA((d,))] * 4
    in_vmem = pl.BlockSpec(memory_space=pltpu.VMEM)
    outputs = pl.pallas_call(
        kernel,
        out_shape=jax.ShapeDtypeStruct((2 * CENTRES, MEMBERS), F32),
        in_specs=[pl.BlockSpec(memory_space=pl.ANY)] * 6,
        out_specs=in_vmem,
        scratch_shapes=scratch,
        compiler_params=pltpu.CompilerParams(
            collective_id=0, has_side_effects=True, vmem_limit_bytes=60 * 1024 * 1024
        ),
        cost_estimate=pl.CostEstimate(flops=3_000_000_000, bytes_accessed=2_000_000, transcendentals=262144),
        name="gauss_newton",
    )(
        sensitivity.reshape(SLOTS, NY, 2, CENTRES, BLOCK), block_list.reshape(1, SLOTS), margin.T, centres,
        controls, observed,
    )
    return outputs[:CENTRES], outputs[CENTRES:]


def solution(mesh):
    return jax.shard_map(
        local,
        mesh=mesh,
        in_specs=(
            P("stn", "cell", None, None, None),
            P("stn", "cell", None),
            P("cell", None),
            P("cell", None),
            P(("stn", "cell"), None),
            P(("stn", "cell"), None),
        ),
        out_specs=(P(("stn", "cell"), None), P(("stn", "cell"), None)),
        check_vma=False,
    )
```

```python
import jax
import jax.numpy as jnp
from jax import lax
from jax.experimental import pallas as pl
from jax.experimental.pallas import tpu as pltpu
from jax.sharding import PartitionSpec as P

MESH = pl.DeviceIdType.MESH
ITERS = 3
SLOTS, BLOCK, MARGINS, CENTRES, MEMBERS = 2, 512, 4, 32, 128
NX, NZ, NY = 4, 8, 8
NSTN, NCELL = NX * NZ, NY * 2
F32, BF16 = jnp.float32, jnp.bfloat16


def split(value):
    high = value.astype(BF16)
    low = (value - high.astype(F32)).astype(BF16)
    return high, low


def column_sum(value):
    return jnp.sum(value.reshape(-1, MEMBERS), axis=0, keepdims=True)


def interleave(first, second):
    upper = lax.broadcasted_iota(jnp.int32, first.shape, 1) < MARGINS
    even = jnp.where(upper, first, pltpu.roll(second, MARGINS, 1))
    odd = jnp.where(upper, pltpu.roll(first, MARGINS, 1), second)
    return even, odd


def kernel(
    sens_hbm, blocks_hbm, margin_hbm, centres_hbm, controls, observed_hbm, outputs,
    blocks, margin, centres, observed, sens, sens_t, basis, basis_r, basis_t, coeff_rhs, cell_rhs, row_rhs, slope, pulled,
    list_in, hits, hot, hot_t, same, entry_rhs,
    gath, part, core_in, paired, y_in, full, scat_out, scat_in, ans_out, ans_in,
    own_grad, own_dir, own_image, own_res, own_upd,
    row_core, row_core_in, row_y, row_y_in, row_s, row_s_in, row_c, row_c_in, row_n, row_n_in, row_m, row_m_in, grad_out, grad_in,
    sens_sem, blocks_sem, margin_sem, centres_sem, controls_sem, observed_sem, li_s, li_r, gz_s, gz_r, gx_s, gx_r, hx_s, hx_r, hz_s, hz_r, cc_s, cc_r,
    c_s, c_r, y_s, y_r, fy_s, fy_r, fc_s, fc_r,
    sc_s, sc_r, an_s, an_r, rc_s, rc_r, ry_s, ry_r, rs_s, rs_r, nx_s, nx_r, nz_s, nz_r, gr_s, gr_r,
):
    stn, cell = lax.axis_index("stn"), lax.axis_index("cell")
    x, z = stn // NZ, stn % NZ
    y, core = cell // 2, cell % 2
    def ring(size, step):
        return min(step, size - step)

    far_y = sorted(range(1, NY), key=lambda d: -ring(NY, d))
    far_z = sorted(range(1, NZ), key=lambda d: -ring(NZ, d))
    far_x = sorted(range(1, NX), key=lambda d: -ring(NX, d))
    far_s = sorted(
        [(a, b) for a in range(NX) for b in range(NZ) if a or b],
        key=lambda d: -ring(NX, d[0]) - ring(NZ, d[1]),
    )
    x_peers = [((x + d) % NX, ((x + d) % NX) * NZ + z, cell) for d in far_x]
    z_peers = [((z + d) % NZ, x * NZ + (z + d) % NZ, cell) for d in far_z]
    y_peers = [((y + d) % NY, stn, ((y + d) % NY) * 2 + core) for d in far_y]
    y_others = [((y + d) % NY, stn, ((y + d) % NY) * 2 + 1 - core) for d in far_y]
    core_peer = (1 - core, stn, y * 2 + 1 - core)
    s_peers = [((x + a) % NX * NZ + (z + b) % NZ, (x + a) % NX * NZ + (z + b) % NZ, cell) for a, b in far_s]

    def send(src, dst, ssem, rsem, peer):
        pltpu.make_async_remote_copy(
            src_ref=src, dst_ref=dst, send_sem=ssem, recv_sem=rsem,
            device_id={"stn": peer[1], "cell": peer[2]}, device_id_type=MESH,
        ).start()

    def drain(ref, sem):
        pltpu.make_async_copy(ref, ref, sem).wait()

    barrier = pltpu.get_barrier_semaphore()
    everyone = z_peers + y_peers + x_peers + [core_peer]
    for peer in everyone:
        pl.semaphore_signal(
            barrier, inc=1, device_id={"stn": peer[1], "cell": peer[2]}, device_id_type=MESH
        )
    first = pltpu.make_async_copy(controls, gath.at[x, z], controls_sem)
    first.start()
    small = [
        pltpu.make_async_copy(src, dst, sem) for src, dst, sem in (
            (blocks_hbm, blocks, blocks_sem), (margin_hbm, margin, margin_sem),
            (centres_hbm, centres, centres_sem), (observed_hbm, observed, observed_sem),
        )
    ]
    for copy in small:
        copy.start()
    for half, side in ((0, 1 - core), (1, core)):
        for n in range(SLOTS):
            for p, d in enumerate(far_y + [0]):
                pltpu.make_async_copy(
                    sens_hbm.at[n, (y + d) % NY, side], sens.at[half, n, p], sens_sem.at[half * SLOTS + n]
                ).start()
    first.wait()
    pl.semaphore_wait(barrier, len(everyone))

    most, rest = pl.ds(0, 24), pl.ds(24, 8)
    for peer in z_peers:
        send(gath.at[x, z, most], gath.at[x, z, most], gz_s, gz_r, peer)
    for peer in x_peers:
        send(gath.at[x, z, rest], gath.at[x, z, rest], hx_s, hx_r, peer)

    for copy in small:
        copy.wait()
    listed = [[margin[o, blocks[0, n]] for o in range(MARGINS)] for n in range(SLOTS)]
    entry = lax.broadcasted_iota(jnp.int32, (1, MEMBERS), 1)
    lists = jnp.zeros((1, MEMBERS), F32)
    for n in range(SLOTS):
        for o in range(MARGINS):
            lists = jnp.where(entry == n * MARGINS + o, listed[n][o].astype(F32), lists)
    list_in[stn] = lists
    grad_out[...] = jnp.zeros_like(grad_out)

    lane = lax.broadcasted_iota(jnp.int32, (8, MEMBERS), 1)
    rows_of_centres = [
        jnp.broadcast_to(centres[0:1, i * MEMBERS:(i + 1) * MEMBERS], (8, MEMBERS)) for i in range(8)
    ]
    to_row = lax.broadcasted_iota(jnp.int32, (MEMBERS, MEMBERS), 0)
    to_col = lax.broadcasted_iota(jnp.int32, (MEMBERS, MEMBERS), 1)
    by_row = (to_row == (to_col % MARGINS) * CENTRES + to_col // MARGINS).astype(BF16)
    for n in range(SLOTS):
        block = blocks[0, n]
        centre = jnp.zeros((8, MEMBERS), jnp.int32)
        for o in range(MARGINS):
            j = listed[n][o]
            row = rows_of_centres[0]
            for i in range(1, 8):
                row = jnp.where(j // 4 == i, rows_of_centres[i], row)
            turned = row
            for i in range(1, 4):
                turned = jnp.where((o + 4 - j % 4) % 4 == i, pltpu.roll(row, i * CENTRES, 1), turned)
            centre = jnp.where(lane // CENTRES == o, turned, centre)
        centre = centre[0:1]
        cells = lax.broadcasted_iota(jnp.int32, (BLOCK, MEMBERS), 0) + block * BLOCK
        squared = jnp.zeros((BLOCK, MEMBERS), F32)
        for shift, mask in ((10, 1048575), (5, 31), (0, 31)):
            cell_coord = ((cells >> shift) & mask).astype(F32)
            centre_coord = ((centre >> shift) & mask).astype(F32)
            spread = cell_coord - centre_coord
            squared = squared + spread * spread
        table = jnp.exp(squared * (-0.5 / 100.0))
        high, low = split(table)
        basis[n, :, 0:MEMBERS] = high
        basis[n, :, MEMBERS:] = low
        high = jnp.dot(high, by_row, preferred_element_type=F32)
        low = jnp.dot(low, by_row, preferred_element_type=F32)
        basis_r[n, :, 0:MEMBERS] = high.astype(BF16)
        basis_r[n, :, MEMBERS:] = low.astype(BF16)
        basis_t[n, 0:MEMBERS] = high.T.astype(BF16)
        basis_t[n, MEMBERS:] = low.T.astype(BF16)

    drain(gath.at[0, 0:NZ - 1, most], gz_r)
    for peer in x_peers:
        send(gath.at[x, :, most], gath.at[x, :, most], gx_s, gx_r, peer)
    drain(gath.at[0:NX - 1, 0, rest], hx_r)
    for peer in z_peers:
        send(gath.at[:, z, rest], gath.at[:, z, rest], hz_s, hz_r, peer)
    for half in range(2):
        for n in range(SLOTS):
            drain(sens.at[half, n], sens_sem.at[half * SLOTS + n])
            for i in range(2):
                piece = sens[half, n, i * 4:(i + 1) * 4].reshape(128, BLOCK)
                sens_t[half, n * BLOCK:(n + 1) * BLOCK, i * 128:(i + 1) * 128] = piece.T
    drain(gath.at[0:NX - 1, :, most], gx_r)
    drain(gath.at[:, 0:NZ - 1, rest], hz_r)

    def send_lists():
        for peer in s_peers:
            send(list_in.at[stn], list_in.at[stn], li_s, li_r, peer)

    def use_lists():
        drain(list_in.at[0:NSTN - 1], li_r)
        everyones = jnp.concatenate([list_in[i] for i in range(NSTN)], axis=0)
        number = lax.broadcasted_iota(jnp.int32, (NSTN, MEMBERS), 1).astype(F32)
        for e in range(SLOTS * MARGINS):
            hits[:, e, :] = (everyones[:, e:e + 1] == number).astype(F32)
        found = hits[...].reshape(NSTN * SLOTS * MARGINS, MEMBERS)
        hot[...] = found.astype(BF16)
        found_t = found.T.astype(BF16)
        hot_t[...] = found_t[0:NSTN]
        same[...] = jnp.dot(hot[...], found_t, preferred_element_type=F32).astype(BF16)

    def times_basis(table, n):
        both = jnp.dot(table[n], coeff_rhs[n], preferred_element_type=F32)
        return both[:, 0:MEMBERS] + both[:, MEMBERS:]

    def put_coeffs(n, at, rows, value):
        high, low = split(value)
        for base in (0, MEMBERS):
            coeff_rhs[n, base + at:base + at + rows, 0:MEMBERS] = high
            coeff_rhs[n, base + at:base + at + rows, MEMBERS:] = low

    def both_ways(left, rhs):
        both = jnp.dot(left, rhs, preferred_element_type=F32)
        return both[:, 0:MEMBERS] + both[:, MEMBERS:]

    def station_rows(half):
        both = jnp.dot(sens[half, 0].reshape(BLOCK // 2, BLOCK), cell_rhs[0], preferred_element_type=F32)
        both += jnp.dot(sens[half, 1].reshape(BLOCK // 2, BLOCK), cell_rhs[1], preferred_element_type=F32)
        return (both[:, 0:MEMBERS] + both[:, MEMBERS:]).reshape(NY, CENTRES, MEMBERS)

    def put_cells(n, value):
        high, low = split(value)
        cell_rhs[n, :, 0:MEMBERS] = high
        cell_rhs[n, :, MEMBERS:] = low

    def share_row(i):
        drain(row_core_in.at[i], rc_r.at[i])
        row_y[i] = row_core[i] + row_core_in[i]
        for peer in y_peers:
            send(row_y.at[i], row_y_in.at[i, y], ry_s.at[i], ry_r.at[i], peer)
        row_y_in[i, y] = row_y[i]

    def shared_row(i):
        drain(row_y_in.at[i, 0:NY - 1], ry_r.at[i])
        return sum(row_y_in[i, j] for j in range(NY))

    groups = (slice(0, 3), slice(3, NY))
    place = {d: p for p, d in enumerate(far_y + [0])}

    def sum_cells(k, group_norm=None, meanwhile=None):
        part[k] = station_rows(0)
        for g, blocks_of in enumerate(groups):
            send(part.at[k, blocks_of], core_in.at[k, blocks_of], c_s.at[2 * k + g], c_r.at[2 * k + g], core_peer)
        own_rows = station_rows(1)
        if group_norm is not None:
            row_core[k] = group_norm()
            send(row_core.at[k], row_core_in.at[k], rc_s.at[k], rc_r.at[k], core_peer)
        for g, blocks_of in enumerate(groups):
            drain(core_in.at[k, blocks_of], c_r.at[2 * k + g])
            paired[k, blocks_of] = own_rows[blocks_of] + core_in[k, blocks_of]
            for p, peer in list(enumerate(y_peers))[blocks_of]:
                send(paired.at[k, p], y_in.at[k, y], y_s.at[k], y_r.at[k], peer)
        y_in[k, y] = paired[k, NY - 1]
        if meanwhile is not None:
            meanwhile()
        norm = None
        if group_norm is not None:
            share_row(k)
            norm = shared_row(k)
        drain(y_in.at[k, 0:NY - 1], y_r.at[k])
        return sum(y_in[k, i] for i in range(NY)), norm

    def gather_cells(k, rows, with_curvature=True):
        full[k, 1, NY - 1] = rows
        for p, peer in enumerate(y_peers):
            g = int(p >= 3)
            send(
                full.at[k, 1, NY - 1], full.at[k, 1, place[NY - far_y[p]]],
                fy_s.at[2 * k + g], fy_r.at[2 * k + g], peer,
            )
        if with_curvature:
            row_s[k] = column_sum(rows * rows)
            for peer in s_peers:
                send(row_s.at[k], row_s_in.at[k, stn], rs_s.at[k], rs_r.at[k], peer)
            row_s_in[k, stn] = row_s[k]

    def pull(half):
        return both_ways(sens_t[half], row_rhs[half]).reshape(SLOTS, BLOCK, MEMBERS)

    def put_rows(half, value):
        high, low = split(value)
        row_rhs[half, :, 0:MEMBERS] = high
        row_rhs[half, :, MEMBERS:] = low

    def adjoint(k, with_curvature):
        for g, arrived in ((1, slice(3, NY - 1)), (0, slice(0, 3))):
            drain(full.at[k, 1, arrived], fy_r.at[2 * k + g])
            send(
                full.at[k, 1, groups[g]], full.at[k, 0, groups[g]],
                fc_s.at[2 * k + g], fc_r.at[2 * k + g], core_peer,
            )
        put_rows(1, full[k, 1].reshape(BLOCK // 2, MEMBERS))
        pulled[...] = pull(1)
        if with_curvature:
            drain(row_s_in.at[k, 0:NSTN - 1], rs_r.at[k])
            row_core[ITERS + k] = sum(row_s_in[k, i] for i in range(NSTN))
            send(row_core.at[ITERS + k], row_core_in.at[ITERS + k], rc_s.at[ITERS + k], rc_r.at[ITERS + k], core_peer)
        for g in (1, 0):
            drain(full.at[k, 0, groups[g]], fc_r.at[2 * k + g])
        put_rows(0, full[k, 0].reshape(BLOCK // 2, MEMBERS))
        rest_of = pull(0)
        for n in range(SLOTS):
            put_cells(n, slope[n] * (pulled[n] + rest_of[n]))
        if with_curvature:
            share_row(ITERS + k)
        parts = []
        for n in range(SLOTS):
            two = both_ways(basis_t[n], cell_rhs[n])
            parts.append((two[0:MEMBERS] + two[MEMBERS:]).reshape(CENTRES // 2, 2 * MARGINS, MEMBERS))
        even, odd = interleave(parts[0], parts[1])
        scat_out[k, :, 0] = even
        scat_out[k, :, 1] = odd
        for peer in s_peers:
            send(scat_out.at[k, peer[0] // 2, peer[0] % 2], scat_in.at[k, stn], sc_s.at[k], sc_r.at[k], peer)
        scat_in[k, stn] = scat_out[k, stn // 2, stn % 2]
        curvature = None
        if with_curvature:
            curvature = shared_row(ITERS + k)
        drain(scat_in.at[k, 0:NSTN - 1], sc_r.at[k])
        high, low = split(scat_in[k].reshape(NSTN * SLOTS * MARGINS, MEMBERS))
        entry_rhs[:, 0:MEMBERS] = high
        entry_rhs[:, MEMBERS:] = low
        return curvature

    def own_change():
        return both_ways(hot_t[...], entry_rhs[...])

    def answer(k, step=None):
        change = both_ways(same[...], entry_rhs[...]).reshape(NSTN, SLOTS * MARGINS, MEMBERS)
        ans_out[k] = change if step is None else ans_out[k - 1] - step * change
        for peer in s_peers:
            send(ans_out.at[k, peer[0]], ans_in.at[k, stn], an_s.at[k], an_r.at[k], peer)
        ans_in[k, stn] = ans_out[k, stn]
        own = own_change() if step is None else own_grad[...] - step * own_change()
        own_grad[...] = own
        row_n[k] = column_sum(own * own)
        for peer in x_peers:
            send(row_n.at[k], row_n_in.at[k, x], nx_s.at[k], nx_r.at[k], peer)
        row_n_in[k, x] = row_n[k]
        for j in range(NSTN):
            grad_out[j, k:k + 1] = own[j:j + 1]
        drain(row_n_in.at[k, 0:NX - 1], nx_r.at[k])
        row_m[k] = sum(row_n_in[k, i] for i in range(NX))
        for peer in z_peers:
            send(row_m.at[k], row_m_in.at[k, z], nz_s.at[k], nz_r.at[k], peer)
        row_m_in[k, z] = row_m[k]
        if k == ITERS - 1:
            for peer in s_peers:
                send(grad_out.at[peer[0]], grad_in.at[stn], gr_s, gr_r, peer)
            grad_in[stn] = grad_out[stn]

    for n in range(SLOTS):
        for o in range(MARGINS):
            put_coeffs(n, o * CENTRES, CENTRES, gath[listed[n][o] // NZ, listed[n][o] % NZ])
        tanh_phi = jnp.tanh(times_basis(basis, n))
        slope[n] = 0.5 * (1.0 - tanh_phi * tanh_phi)
        put_cells(n, 0.5 * (1.0 + tanh_phi))
    predicted, _ = sum_cells(0, meanwhile=send_lists)
    own_res[...] = observed[...] - predicted
    gather_cells(0, own_res[...], False)
    use_lists()
    adjoint(0, False)
    answer(0)

    norm, ratios, steps = None, [], []
    for k in range(1, ITERS + 1):
        drain(ans_in.at[k - 1, 0:NSTN - 1], an_r.at[k - 1])
        tiles = ans_in[k - 1].reshape(CENTRES // 2, 2, SLOTS * MARGINS, MEMBERS)
        for n, tile in enumerate(interleave(tiles[:, 0], tiles[:, 1])):
            put_coeffs(n, 0, MEMBERS, tile.reshape(MEMBERS, MEMBERS))
        fields = [times_basis(basis_r, n) for n in range(SLOTS)]
        for n in range(SLOTS):
            put_cells(n, slope[n] * fields[n])

        def group_norm():
            drain(row_m_in.at[k - 1, 0:NZ - 1], nz_r.at[k - 1])
            return sum(row_m_in[k - 1, i] for i in range(NZ))

        image, new_norm = sum_cells(k, group_norm)
        ratio = new_norm / norm if k > 1 else None
        if k > 1:
            image = image + ratio * own_image[...]
        norm = new_norm
        own_image[...] = image
        if k < ITERS:
            gather_cells(k, image)
        else:
            row_c[...] = column_sum(image * image)
            for peer in y_others + y_peers + [core_peer]:
                send(row_c, row_c_in.at[cell], cc_s, cc_r, peer)
        ratios.append(ratio)
        if k < ITERS:
            curvature = adjoint(k, True)
            step = norm / curvature
            answer(k, step)
        else:
            row_c_in[cell] = row_c[...]
            drain(grad_in.at[0:NSTN - 1], gr_r)
            for i in range(ITERS):
                direction = jnp.concatenate([grad_in[t, i:i + 1] for t in range(NSTN)], axis=0)
                if i > 0:
                    direction = direction + ratios[i] * own_dir[...]
                own_dir[...] = direction
                if i < ITERS - 1:
                    own_upd[...] = steps[i] * direction if i == 0 else own_upd[...] + steps[i] * direction
            drain(row_c_in.at[0:NCELL - 1], cc_r)
            row_s[0] = sum(row_c_in[i] for i in range(NCELL))
            for peer in s_peers:
                send(row_s.at[0], row_s_in.at[0, stn], rs_s.at[0], rs_r.at[0], peer)
            row_s_in[0, stn] = row_s[0]
            drain(row_s_in.at[0, 0:NSTN - 1], rs_r.at[0])
            step = norm / sum(row_s_in[0, i] for i in range(NSTN))
        own_res[...] = own_res[...] - step * image
        steps.append(step)

    outputs[0:CENTRES] = gath[x, z] + (own_upd[...] + steps[-1] * own_dir[...])
    outputs[CENTRES:] = own_res[...]

    drain(gath.at[0, 0:NZ - 1, most], gz_s)
    drain(gath.at[0:NX - 1, :, most], gx_s)
    drain(gath.at[0:NX - 1, 0, rest], hx_s)
    drain(gath.at[:, 0:NZ - 1, rest], hz_s)
    drain(row_c_in.at[0:NCELL - 1], cc_s)
    drain(grad_in.at[0:NSTN - 1], gr_s)
    drain(list_in.at[0:NSTN - 1], li_s)
    for k in range(ITERS + 1):
        for g in range(2):
            drain(core_in.at[k, groups[g]], c_s.at[2 * k + g])
        drain(y_in.at[k, 0:NY - 1], y_s.at[k])
    for k in range(1, 2 * ITERS):
        drain(row_core_in.at[k], rc_s.at[k])
        drain(row_y_in.at[k, 0:NY - 1], ry_s.at[k])
    for k in range(ITERS):
        for g, arrived in ((1, slice(3, NY - 1)), (0, slice(0, 3))):
            drain(full.at[k, 1, arrived], fy_s.at[2 * k + g])
            drain(full.at[k, 0, groups[g]], fc_s.at[2 * k + g])
        drain(scat_in.at[k, 0:NSTN - 1], sc_s.at[k])
        drain(ans_in.at[k, 0:NSTN - 1], an_s.at[k])
        drain(row_s_in.at[k, 0:NSTN - 1], rs_s.at[k])
        drain(row_n_in.at[k, 0:NX - 1], nx_s.at[k])
        drain(row_m_in.at[k, 0:NZ - 1], nz_s.at[k])


def local(sensitivity, block_list, margin, centres, controls, observed):
    rows = (CENTRES, MEMBERS)
    a, d, r = ITERS + 1, ITERS, 2 * ITERS

    def vmem(*shape):
        return pltpu.VMEM(shape, F32)

    entries = SLOTS * MARGINS
    scratch = [
        pltpu.SMEM((1, SLOTS), jnp.int32),
        pltpu.SMEM((MARGINS, margin.shape[0]), jnp.int32),
        pltpu.VMEM(centres.shape, jnp.int32),
        vmem(*rows),
        pltpu.VMEM((2, SLOTS, NY, CENTRES, BLOCK), BF16),
        pltpu.VMEM((2, SLOTS * BLOCK, BLOCK // 2), BF16),
        pltpu.VMEM((SLOTS, BLOCK, 2 * MEMBERS), BF16),
        pltpu.VMEM((SLOTS, BLOCK, 2 * MEMBERS), BF16),
        pltpu.VMEM((SLOTS, 2 * MEMBERS, BLOCK), BF16),
        pltpu.VMEM((SLOTS, 2 * MEMBERS, 2 * MEMBERS), BF16),
        pltpu.VMEM((SLOTS, BLOCK, 2 * MEMBERS), BF16),
        pltpu.VMEM((2, BLOCK // 2, 2 * MEMBERS), BF16),
        vmem(SLOTS, BLOCK, MEMBERS),
        vmem(SLOTS, BLOCK, MEMBERS),
        vmem(NSTN, 1, MEMBERS),
        vmem(NSTN, entries, MEMBERS),
        pltpu.VMEM((NSTN * entries, MEMBERS), BF16),
        pltpu.VMEM((NSTN, NSTN * entries), BF16),
        pltpu.VMEM((NSTN * entries, NSTN * entries), BF16),
        pltpu.VMEM((NSTN * entries, 2 * MEMBERS), BF16),
        vmem(NX, NZ, *rows),
        vmem(a, NY, *rows),
        vmem(a, NY, *rows),
        vmem(a, NY, *rows),
        vmem(a, NY, *rows),
        vmem(d, 2, NY, *rows),
        vmem(d, CENTRES // 2, 2, entries, MEMBERS),
        vmem(d, NSTN, entries, MEMBERS),
        vmem(d, NSTN, entries, MEMBERS),
        vmem(d, NSTN, entries, MEMBERS),
        vmem(*rows), vmem(*rows), vmem(*rows), vmem(*rows), vmem(*rows),
        vmem(r, 1, MEMBERS), vmem(r, 1, MEMBERS),
        vmem(r, 1, MEMBERS), vmem(r, NY, 1, MEMBERS),
        vmem(d, 1, MEMBERS), vmem(d, NSTN, 1, MEMBERS),
        vmem(1, MEMBERS), vmem(NCELL, 1, MEMBERS),
        vmem(d, 1, MEMBERS), vmem(d, NX, 1, MEMBERS),
        vmem(d, 1, MEMBERS), vmem(d, NZ, 1, MEMBERS),
        vmem(NSTN, d + 1, MEMBERS), vmem(NSTN, d + 1, MEMBERS),
    ]
    scratch += [pltpu.SemaphoreType.DMA((2 * SLOTS,))]
    scratch += [pltpu.SemaphoreType.DMA] * 17
    scratch += [pltpu.SemaphoreType.DMA((2 * a,))] * 2
    scratch += [pltpu.SemaphoreType.DMA((a,))] * 2
    scratch += [pltpu.SemaphoreType.DMA((2 * d,))] * 4
    scratch += [pltpu.SemaphoreType.DMA((d,))] * 4
    scratch += [pltpu.SemaphoreType.DMA((r,))] * 4
    scratch += [pltpu.SemaphoreType.DMA((d,))] * 6
    scratch += [pltpu.SemaphoreType.DMA] * 2
    in_vmem = pl.BlockSpec(memory_space=pltpu.VMEM)
    outputs = pl.pallas_call(
        kernel,
        out_shape=jax.ShapeDtypeStruct((2 * CENTRES, MEMBERS), F32),
        in_specs=[pl.BlockSpec(memory_space=pl.ANY)] * 6,
        out_specs=in_vmem,
        scratch_shapes=scratch,
        compiler_params=pltpu.CompilerParams(
            collective_id=0, has_side_effects=True, vmem_limit_bytes=60 * 1024 * 1024
        ),
        cost_estimate=pl.CostEstimate(flops=3_000_000_000, bytes_accessed=2_000_000, transcendentals=262144),
        name="gauss_newton",
    )(
        sensitivity.reshape(SLOTS, NY, 2, CENTRES, BLOCK), block_list.reshape(1, SLOTS), margin.T, centres,
        controls, observed,
    )
    return outputs[:CENTRES], outputs[CENTRES:]


def solution(mesh):
    return jax.shard_map(
        local,
        mesh=mesh,
        in_specs=(
            P("stn", "cell", None, None, None),
            P("stn", "cell", None),
            P("cell", None),
            P("cell", None),
            P(("stn", "cell"), None),
            P(("stn", "cell"), None),
        ),
        out_specs=(P(("stn", "cell"), None), P(("stn", "cell"), None)),
        check_vma=False,
    )
```

```python
import jax
import jax.numpy as jnp
from jax import lax
from jax.experimental import pallas as pl
from jax.experimental.pallas import tpu as pltpu
from jax.sharding import PartitionSpec as P

MESH = pl.DeviceIdType.MESH
ITERS = 3
SLOTS, BLOCK, MARGINS, CENTRES, MEMBERS = 2, 512, 4, 32, 128
NX, NZ, NY = 4, 8, 8
NSTN, NCELL = NX * NZ, NY * 2
F32, BF16 = jnp.float32, jnp.bfloat16


def split(value):
    high = value.astype(BF16)
    low = (value - high.astype(F32)).astype(BF16)
    return high, low


def wide(value):
    return jnp.concatenate(split(value), axis=1)


def column_sum(value):
    return jnp.sum(value.reshape(-1, MEMBERS), axis=0, keepdims=True)


def interleave(first, second):
    upper = lax.broadcasted_iota(jnp.int32, first.shape, 1) < MARGINS
    even = jnp.where(upper, first, pltpu.roll(second, MARGINS, 1))
    odd = jnp.where(upper, pltpu.roll(first, MARGINS, 1), second)
    return even, odd


def kernel(
    sens_hbm, blocks_hbm, margin_hbm, centres_hbm, controls, observed_hbm, outputs,
    blocks, margin, centres, observed, sens, sens_t, basis, basis_r, basis_t, coeff_rhs, cell_rhs, slope, pulled,
    list_in, hits, hot, hot_t, same, entry_rhs,
    gath, part, core_in, paired, y_in, full, scat_out, scat_in, ans_out, ans_in,
    own_grad, own_dir, own_image, own_res, own_upd,
    row_core, row_core_in, row_y, row_y_in, row_s, row_s_in, row_c, row_c_in, row_n, row_n_in, row_m, row_m_in, grad_out, grad_in,
    sens_sem, blocks_sem, margin_sem, centres_sem, controls_sem, observed_sem, li_s, li_r, gz_s, gz_r, gx_s, gx_r, hx_s, hx_r, hz_s, hz_r, cc_s, cc_r,
    c_s, c_r, y_s, y_r, fy_s, fy_r, fc_s, fc_r,
    sc_s, sc_r, an_s, an_r, rc_s, rc_r, ry_s, ry_r, rs_s, rs_r, nx_s, nx_r, nz_s, nz_r, gr_s, gr_r,
):
    stn, cell = lax.axis_index("stn"), lax.axis_index("cell")
    x, z = stn // NZ, stn % NZ
    y, core = cell // 2, cell % 2
    def ring(size, step):
        return min(step, size - step)

    far_y = sorted(range(1, NY), key=lambda d: -ring(NY, d))
    far_z = sorted(range(1, NZ), key=lambda d: -ring(NZ, d))
    far_x = sorted(range(1, NX), key=lambda d: -ring(NX, d))
    far_s = sorted(
        [(a, b) for a in range(NX) for b in range(NZ) if a or b],
        key=lambda d: -ring(NX, d[0]) - ring(NZ, d[1]),
    )
    x_peers = [((x + d) % NX, ((x + d) % NX) * NZ + z, cell) for d in far_x]
    z_peers = [((z + d) % NZ, x * NZ + (z + d) % NZ, cell) for d in far_z]
    y_peers = [((y + d) % NY, stn, ((y + d) % NY) * 2 + core) for d in far_y]
    y_others = [((y + d) % NY, stn, ((y + d) % NY) * 2 + 1 - core) for d in far_y]
    core_peer = (1 - core, stn, y * 2 + 1 - core)
    s_peers = [((x + a) % NX * NZ + (z + b) % NZ, (x + a) % NX * NZ + (z + b) % NZ, cell) for a, b in far_s]

    def send(src, dst, ssem, rsem, peer):
        pltpu.make_async_remote_copy(
            src_ref=src, dst_ref=dst, send_sem=ssem, recv_sem=rsem,
            device_id={"stn": peer[1], "cell": peer[2]}, device_id_type=MESH,
        ).start()

    def drain(ref, sem):
        pltpu.make_async_copy(ref, ref, sem).wait()

    barrier = pltpu.get_barrier_semaphore()
    everyone = z_peers + y_peers + x_peers + [core_peer]
    for peer in everyone:
        pl.semaphore_signal(
            barrier, inc=1, device_id={"stn": peer[1], "cell": peer[2]}, device_id_type=MESH
        )
    first = pltpu.make_async_copy(controls, gath.at[x, z], controls_sem)
    first.start()
    small = [
        pltpu.make_async_copy(src, dst, sem) for src, dst, sem in (
            (blocks_hbm, blocks, blocks_sem), (margin_hbm, margin, margin_sem),
            (centres_hbm, centres, centres_sem), (observed_hbm, observed, observed_sem),
        )
    ]
    for copy in small:
        copy.start()
    for half, side in ((0, 1 - core), (1, core)):
        for n in range(SLOTS):
            for p, d in enumerate(far_y + [0]):
                pltpu.make_async_copy(
                    sens_hbm.at[n, (y + d) % NY, side], sens.at[half, n, p], sens_sem.at[half * SLOTS + n]
                ).start()
    first.wait()
    pl.semaphore_wait(barrier, len(everyone))

    most, rest = pl.ds(0, 24), pl.ds(24, 8)
    for peer in z_peers:
        send(gath.at[x, z, most], gath.at[x, z, most], gz_s, gz_r, peer)
    for peer in x_peers:
        send(gath.at[x, z, rest], gath.at[x, z, rest], hx_s, hx_r, peer)

    for copy in small:
        copy.wait()
    listed = [[margin[o, blocks[0, n]] for o in range(MARGINS)] for n in range(SLOTS)]
    entry = lax.broadcasted_iota(jnp.int32, (1, MEMBERS), 1)
    lists = jnp.zeros((1, MEMBERS), F32)
    for n in range(SLOTS):
        for o in range(MARGINS):
            lists = jnp.where(entry == n * MARGINS + o, listed[n][o].astype(F32), lists)
    list_in[stn] = lists
    grad_out[...] = jnp.zeros_like(grad_out)

    lane = lax.broadcasted_iota(jnp.int32, (8, MEMBERS), 1)
    rows_of_centres = [
        jnp.broadcast_to(centres[0:1, i * MEMBERS:(i + 1) * MEMBERS], (8, MEMBERS)) for i in range(8)
    ]
    to_row = lax.broadcasted_iota(jnp.int32, (MEMBERS, MEMBERS), 0)
    to_col = lax.broadcasted_iota(jnp.int32, (MEMBERS, MEMBERS), 1)
    by_row = (to_row == (to_col % MARGINS) * CENTRES + to_col // MARGINS).astype(BF16)
    for n in range(SLOTS):
        block = blocks[0, n]
        centre = jnp.zeros((8, MEMBERS), jnp.int32)
        for o in range(MARGINS):
            j = listed[n][o]
            row = rows_of_centres[0]
            for i in range(1, 8):
                row = jnp.where(j // 4 == i, rows_of_centres[i], row)
            turned = row
            for i in range(1, 4):
                turned = jnp.where((o + 4 - j % 4) % 4 == i, pltpu.roll(row, i * CENTRES, 1), turned)
            centre = jnp.where(lane // CENTRES == o, turned, centre)
        centre = centre[0:1]
        cells = lax.broadcasted_iota(jnp.int32, (BLOCK, MEMBERS), 0) + block * BLOCK
        squared = jnp.zeros((BLOCK, MEMBERS), F32)
        for shift, mask in ((10, 1048575), (5, 31), (0, 31)):
            cell_coord = ((cells >> shift) & mask).astype(F32)
            centre_coord = ((centre >> shift) & mask).astype(F32)
            spread = cell_coord - centre_coord
            squared = squared + spread * spread
        table = jnp.exp(squared * (-0.5 / 100.0))
        high, low = split(table)
        basis[n, :, 0:MEMBERS] = high
        basis[n, :, MEMBERS:] = low
        high = jnp.dot(high, by_row, preferred_element_type=F32)
        low = jnp.dot(low, by_row, preferred_element_type=F32)
        basis_r[n, :, 0:MEMBERS] = high.astype(BF16)
        basis_r[n, :, MEMBERS:] = low.astype(BF16)
        basis_t[n, 0:MEMBERS] = high.T.astype(BF16)
        basis_t[n, MEMBERS:] = low.T.astype(BF16)

    drain(gath.at[0, 0:NZ - 1, most], gz_r)
    for peer in x_peers:
        send(gath.at[x, :, most], gath.at[x, :, most], gx_s, gx_r, peer)
    drain(gath.at[0:NX - 1, 0, rest], hx_r)
    for peer in z_peers:
        send(gath.at[:, z, rest], gath.at[:, z, rest], hz_s, hz_r, peer)
    for half in range(2):
        for n in range(SLOTS):
            drain(sens.at[half, n], sens_sem.at[half * SLOTS + n])
            for i in range(2):
                piece = sens[half, n, i * 4:(i + 1) * 4].reshape(128, BLOCK)
                sens_t[half, n * BLOCK:(n + 1) * BLOCK, i * 128:(i + 1) * 128] = piece.T
    drain(gath.at[0:NX - 1, :, most], gx_r)
    drain(gath.at[:, 0:NZ - 1, rest], hz_r)

    def send_lists():
        for peer in s_peers:
            send(list_in.at[stn], list_in.at[stn], li_s, li_r, peer)

    def use_lists():
        drain(list_in.at[0:NSTN - 1], li_r)
        everyones = jnp.concatenate([list_in[i] for i in range(NSTN)], axis=0)
        number = lax.broadcasted_iota(jnp.int32, (NSTN, MEMBERS), 1).astype(F32)
        for e in range(SLOTS * MARGINS):
            hits[:, e, :] = (everyones[:, e:e + 1] == number).astype(F32)
        found = hits[...].reshape(NSTN * SLOTS * MARGINS, MEMBERS)
        hot[...] = found.astype(BF16)
        found_t = found.T.astype(BF16)
        hot_t[...] = found_t[0:NSTN]
        same[...] = jnp.dot(hot[...], found_t, preferred_element_type=F32).astype(BF16)

    def times_basis(table, n):
        both = jnp.dot(table[n], coeff_rhs[n], preferred_element_type=F32)
        return both[:, 0:MEMBERS] + both[:, MEMBERS:]

    def put_coeffs(n, at, rows, value):
        high, low = split(value)
        for base in (0, MEMBERS):
            coeff_rhs[n, base + at:base + at + rows, 0:MEMBERS] = high
            coeff_rhs[n, base + at:base + at + rows, MEMBERS:] = low

    def both_ways(left, rhs):
        both = jnp.dot(left, rhs, preferred_element_type=F32)
        return both[:, 0:MEMBERS] + both[:, MEMBERS:]

    def station_rows(half, at=slice(0, NY)):
        count = (at.stop - at.start) * CENTRES
        both = jnp.dot(sens[half, 0, at].reshape(count, BLOCK), cell_rhs[0], preferred_element_type=F32)
        both += jnp.dot(sens[half, 1, at].reshape(count, BLOCK), cell_rhs[1], preferred_element_type=F32)
        return (both[:, 0:MEMBERS] + both[:, MEMBERS:]).reshape(-1, CENTRES, MEMBERS)

    def put_cells(n, value):
        high, low = split(value)
        cell_rhs[n, :, 0:MEMBERS] = high
        cell_rhs[n, :, MEMBERS:] = low

    def share_row(i):
        drain(row_core_in.at[i], rc_r.at[i])
        row_y[i] = row_core[i] + row_core_in[i]
        for peer in y_peers:
            send(row_y.at[i], row_y_in.at[i, y], ry_s.at[i], ry_r.at[i], peer)
        row_y_in[i, y] = row_y[i]

    def shared_row(i):
        drain(row_y_in.at[i, 0:NY - 1], ry_r.at[i])
        return sum(row_y_in[i, j] for j in range(NY))

    groups = (slice(0, 3), slice(3, NY))
    place = {d: p for p, d in enumerate(far_y + [0])}

    def sum_cells(k, group_norm=None, meanwhile=None):
        for g, blocks_of in enumerate(groups):
            part[k, blocks_of] = station_rows(0, blocks_of)
            send(part.at[k, blocks_of], core_in.at[k, blocks_of], c_s.at[2 * k + g], c_r.at[2 * k + g], core_peer)
        own_rows = station_rows(1)
        if group_norm is not None:
            row_core[k] = group_norm()
            send(row_core.at[k], row_core_in.at[k], rc_s.at[k], rc_r.at[k], core_peer)
        for g, blocks_of in enumerate(groups):
            drain(core_in.at[k, blocks_of], c_r.at[2 * k + g])
            paired[k, blocks_of] = own_rows[blocks_of] + core_in[k, blocks_of]
            for p, peer in list(enumerate(y_peers))[blocks_of]:
                send(paired.at[k, p], y_in.at[k, y], y_s.at[k], y_r.at[k], peer)
        y_in[k, y] = paired[k, NY - 1]
        if meanwhile is not None:
            meanwhile()
        norm = None
        if group_norm is not None:
            share_row(k)
            norm = shared_row(k)
        drain(y_in.at[k, 0:NY - 1], y_r.at[k])
        return sum(y_in[k, i] for i in range(NY)), norm

    def gather_cells(k, rows, with_curvature=True):
        full[k, 1, NY - 1] = rows
        for p, peer in enumerate(y_peers):
            g = int(p >= 3)
            send(
                full.at[k, 1, NY - 1], full.at[k, 1, place[NY - far_y[p]]],
                fy_s.at[2 * k + g], fy_r.at[2 * k + g], peer,
            )
        if with_curvature:
            row_s[k] = column_sum(rows * rows)
            for peer in s_peers:
                send(row_s.at[k], row_s_in.at[k, stn], rs_s.at[k], rs_r.at[k], peer)
            row_s_in[k, stn] = row_s[k]

    def pull(half, rows):
        return both_ways(sens_t[half], wide(rows)).reshape(SLOTS, BLOCK, MEMBERS)

    def adjoint(k, with_curvature):
        for g, arrived in ((1, slice(3, NY - 1)), (0, slice(0, 3))):
            drain(full.at[k, 1, arrived], fy_r.at[2 * k + g])
            send(
                full.at[k, 1, groups[g]], full.at[k, 0, groups[g]],
                fc_s.at[2 * k + g], fc_r.at[2 * k + g], core_peer,
            )
        pulled[...] = pull(1, full[k, 1].reshape(BLOCK // 2, MEMBERS))
        if with_curvature:
            drain(row_s_in.at[k, 0:NSTN - 1], rs_r.at[k])
            row_core[ITERS + k] = sum(row_s_in[k, i] for i in range(NSTN))
            send(row_core.at[ITERS + k], row_core_in.at[ITERS + k], rc_s.at[ITERS + k], rc_r.at[ITERS + k], core_peer)
        for g in (1, 0):
            drain(full.at[k, 0, groups[g]], fc_r.at[2 * k + g])
        rest_of = pull(0, full[k, 0].reshape(BLOCK // 2, MEMBERS))
        weighted = [wide(slope[n] * (pulled[n] + rest_of[n])) for n in range(SLOTS)]
        if with_curvature:
            share_row(ITERS + k)
        parts = []
        for n in range(SLOTS):
            two = both_ways(basis_t[n], weighted[n])
            parts.append((two[0:MEMBERS] + two[MEMBERS:]).reshape(CENTRES // 2, 2 * MARGINS, MEMBERS))
        even, odd = interleave(parts[0], parts[1])
        scat_out[k, :, 0] = even
        scat_out[k, :, 1] = odd
        for peer in s_peers:
            send(scat_out.at[k, peer[0] // 2, peer[0] % 2], scat_in.at[k, stn], sc_s.at[k], sc_r.at[k], peer)
        scat_in[k, stn] = scat_out[k, stn // 2, stn % 2]
        curvature = None
        if with_curvature:
            curvature = shared_row(ITERS + k)
        drain(scat_in.at[k, 0:NSTN - 1], sc_r.at[k])
        high, low = split(scat_in[k].reshape(NSTN * SLOTS * MARGINS, MEMBERS))
        entry_rhs[:, 0:MEMBERS] = high
        entry_rhs[:, MEMBERS:] = low
        return curvature

    def own_change():
        return both_ways(hot_t[...], entry_rhs[...])

    def answer(k, step=None):
        change = both_ways(same[...], entry_rhs[...]).reshape(NSTN, SLOTS * MARGINS, MEMBERS)
        ans_out[k] = change if step is None else ans_out[k - 1] - step * change
        for peer in s_peers:
            send(ans_out.at[k, peer[0]], ans_in.at[k, stn], an_s.at[k], an_r.at[k], peer)
        ans_in[k, stn] = ans_out[k, stn]
        own = own_change() if step is None else own_grad[...] - step * own_change()
        own_grad[...] = own
        row_n[k] = column_sum(own * own)
        for peer in x_peers:
            send(row_n.at[k], row_n_in.at[k, x], nx_s.at[k], nx_r.at[k], peer)
        row_n_in[k, x] = row_n[k]
        for j in range(NSTN):
            grad_out[j, k:k + 1] = own[j:j + 1]
        drain(row_n_in.at[k, 0:NX - 1], nx_r.at[k])
        row_m[k] = sum(row_n_in[k, i] for i in range(NX))
        for peer in z_peers:
            send(row_m.at[k], row_m_in.at[k, z], nz_s.at[k], nz_r.at[k], peer)
        row_m_in[k, z] = row_m[k]
        if k == ITERS - 1:
            for peer in s_peers:
                send(grad_out.at[peer[0]], grad_in.at[stn], gr_s, gr_r, peer)
            grad_in[stn] = grad_out[stn]

    for n in range(SLOTS):
        for o in range(MARGINS):
            put_coeffs(n, o * CENTRES, CENTRES, gath[listed[n][o] // NZ, listed[n][o] % NZ])
        tanh_phi = jnp.tanh(times_basis(basis, n))
        slope[n] = 0.5 * (1.0 - tanh_phi * tanh_phi)
        put_cells(n, 0.5 * (1.0 + tanh_phi))
    predicted, _ = sum_cells(0, meanwhile=send_lists)
    own_res[...] = observed[...] - predicted
    gather_cells(0, own_res[...], False)
    use_lists()
    adjoint(0, False)
    answer(0)

    norm, ratios, steps = None, [], []
    for k in range(1, ITERS + 1):
        drain(ans_in.at[k - 1, 0:NSTN - 1], an_r.at[k - 1])
        tiles = ans_in[k - 1].reshape(CENTRES // 2, 2, SLOTS * MARGINS, MEMBERS)
        for n, tile in enumerate(interleave(tiles[:, 0], tiles[:, 1])):
            put_coeffs(n, 0, MEMBERS, tile.reshape(MEMBERS, MEMBERS))
        fields = [times_basis(basis_r, n) for n in range(SLOTS)]
        for n in range(SLOTS):
            put_cells(n, slope[n] * fields[n])

        def group_norm():
            drain(row_m_in.at[k - 1, 0:NZ - 1], nz_r.at[k - 1])
            return sum(row_m_in[k - 1, i] for i in range(NZ))

        image, new_norm = sum_cells(k, group_norm)
        ratio = new_norm / norm if k > 1 else None
        if k > 1:
            image = image + ratio * own_image[...]
        norm = new_norm
        own_image[...] = image
        if k < ITERS:
            gather_cells(k, image)
        else:
            row_c[...] = column_sum(image * image)
            for peer in y_others + y_peers + [core_peer]:
                send(row_c, row_c_in.at[cell], cc_s, cc_r, peer)
        ratios.append(ratio)
        if k < ITERS:
            curvature = adjoint(k, True)
            step = norm / curvature
            answer(k, step)
        else:
            row_c_in[cell] = row_c[...]
            drain(grad_in.at[0:NSTN - 1], gr_r)
            for i in range(ITERS):
                direction = jnp.concatenate([grad_in[t, i:i + 1] for t in range(NSTN)], axis=0)
                if i > 0:
                    direction = direction + ratios[i] * own_dir[...]
                own_dir[...] = direction
                if i < ITERS - 1:
                    own_upd[...] = steps[i] * direction if i == 0 else own_upd[...] + steps[i] * direction
            drain(row_c_in.at[0:NCELL - 1], cc_r)
            row_s[0] = sum(row_c_in[i] for i in range(NCELL))
            for peer in s_peers:
                send(row_s.at[0], row_s_in.at[0, stn], rs_s.at[0], rs_r.at[0], peer)
            row_s_in[0, stn] = row_s[0]
            drain(row_s_in.at[0, 0:NSTN - 1], rs_r.at[0])
            step = norm / sum(row_s_in[0, i] for i in range(NSTN))
        own_res[...] = own_res[...] - step * image
        steps.append(step)

    outputs[0:CENTRES] = gath[x, z] + (own_upd[...] + steps[-1] * own_dir[...])
    outputs[CENTRES:] = own_res[...]

    drain(gath.at[0, 0:NZ - 1, most], gz_s)
    drain(gath.at[0:NX - 1, :, most], gx_s)
    drain(gath.at[0:NX - 1, 0, rest], hx_s)
    drain(gath.at[:, 0:NZ - 1, rest], hz_s)
    drain(row_c_in.at[0:NCELL - 1], cc_s)
    drain(grad_in.at[0:NSTN - 1], gr_s)
    drain(list_in.at[0:NSTN - 1], li_s)
    for k in range(ITERS + 1):
        for g in range(2):
            drain(core_in.at[k, groups[g]], c_s.at[2 * k + g])
        drain(y_in.at[k, 0:NY - 1], y_s.at[k])
    for k in range(1, 2 * ITERS):
        drain(row_core_in.at[k], rc_s.at[k])
        drain(row_y_in.at[k, 0:NY - 1], ry_s.at[k])
    for k in range(ITERS):
        for g, arrived in ((1, slice(3, NY - 1)), (0, slice(0, 3))):
            drain(full.at[k, 1, arrived], fy_s.at[2 * k + g])
            drain(full.at[k, 0, groups[g]], fc_s.at[2 * k + g])
        drain(scat_in.at[k, 0:NSTN - 1], sc_s.at[k])
        drain(ans_in.at[k, 0:NSTN - 1], an_s.at[k])
        drain(row_s_in.at[k, 0:NSTN - 1], rs_s.at[k])
        drain(row_n_in.at[k, 0:NX - 1], nx_s.at[k])
        drain(row_m_in.at[k, 0:NZ - 1], nz_s.at[k])


def local(sensitivity, block_list, margin, centres, controls, observed):
    rows = (CENTRES, MEMBERS)
    a, d, r = ITERS + 1, ITERS, 2 * ITERS

    def vmem(*shape):
        return pltpu.VMEM(shape, F32)

    entries = SLOTS * MARGINS
    scratch = [
        pltpu.SMEM((1, SLOTS), jnp.int32),
        pltpu.SMEM((MARGINS, margin.shape[0]), jnp.int32),
        pltpu.VMEM(centres.shape, jnp.int32),
        vmem(*rows),
        pltpu.VMEM((2, SLOTS, NY, CENTRES, BLOCK), BF16),
        pltpu.VMEM((2, SLOTS * BLOCK, BLOCK // 2), BF16),
        pltpu.VMEM((SLOTS, BLOCK, 2 * MEMBERS), BF16),
        pltpu.VMEM((SLOTS, BLOCK, 2 * MEMBERS), BF16),
        pltpu.VMEM((SLOTS, 2 * MEMBERS, BLOCK), BF16),
        pltpu.VMEM((SLOTS, 2 * MEMBERS, 2 * MEMBERS), BF16),
        pltpu.VMEM((SLOTS, BLOCK, 2 * MEMBERS), BF16),
        vmem(SLOTS, BLOCK, MEMBERS),
        vmem(SLOTS, BLOCK, MEMBERS),
        vmem(NSTN, 1, MEMBERS),
        vmem(NSTN, entries, MEMBERS),
        pltpu.VMEM((NSTN * entries, MEMBERS), BF16),
        pltpu.VMEM((NSTN, NSTN * entries), BF16),
        pltpu.VMEM((NSTN * entries, NSTN * entries), BF16),
        pltpu.VMEM((NSTN * entries, 2 * MEMBERS), BF16),
        vmem(NX, NZ, *rows),
        vmem(a, NY, *rows),
        vmem(a, NY, *rows),
        vmem(a, NY, *rows),
        vmem(a, NY, *rows),
        vmem(d, 2, NY, *rows),
        vmem(d, CENTRES // 2, 2, entries, MEMBERS),
        vmem(d, NSTN, entries, MEMBERS),
        vmem(d, NSTN, entries, MEMBERS),
        vmem(d, NSTN, entries, MEMBERS),
        vmem(*rows), vmem(*rows), vmem(*rows), vmem(*rows), vmem(*rows),
        vmem(r, 1, MEMBERS), vmem(r, 1, MEMBERS),
        vmem(r, 1, MEMBERS), vmem(r, NY, 1, MEMBERS),
        vmem(d, 1, MEMBERS), vmem(d, NSTN, 1, MEMBERS),
        vmem(1, MEMBERS), vmem(NCELL, 1, MEMBERS),
        vmem(d, 1, MEMBERS), vmem(d, NX, 1, MEMBERS),
        vmem(d, 1, MEMBERS), vmem(d, NZ, 1, MEMBERS),
        vmem(NSTN, d + 1, MEMBERS), vmem(NSTN, d + 1, MEMBERS),
    ]
    scratch += [pltpu.SemaphoreType.DMA((2 * SLOTS,))]
    scratch += [pltpu.SemaphoreType.DMA] * 17
    scratch += [pltpu.SemaphoreType.DMA((2 * a,))] * 2
    scratch += [pltpu.SemaphoreType.DMA((a,))] * 2
    scratch += [pltpu.SemaphoreType.DMA((2 * d,))] * 4
    scratch += [pltpu.SemaphoreType.DMA((d,))] * 4
    scratch += [pltpu.SemaphoreType.DMA((r,))] * 4
    scratch += [pltpu.SemaphoreType.DMA((d,))] * 6
    scratch += [pltpu.SemaphoreType.DMA] * 2
    in_vmem = pl.BlockSpec(memory_space=pltpu.VMEM)
    outputs = pl.pallas_call(
        kernel,
        out_shape=jax.ShapeDtypeStruct((2 * CENTRES, MEMBERS), F32),
        in_specs=[pl.BlockSpec(memory_space=pl.ANY)] * 6,
        out_specs=in_vmem,
        scratch_shapes=scratch,
        compiler_params=pltpu.CompilerParams(
            collective_id=0, has_side_effects=True, vmem_limit_bytes=60 * 1024 * 1024
        ),
        cost_estimate=pl.CostEstimate(flops=3_000_000_000, bytes_accessed=2_000_000, transcendentals=262144),
        name="gauss_newton",
    )(
        sensitivity.reshape(SLOTS, NY, 2, CENTRES, BLOCK), block_list.reshape(1, SLOTS), margin.T, centres,
        controls, observed,
    )
    return outputs[:CENTRES], outputs[CENTRES:]


def solution(mesh):
    return jax.shard_map(
        local,
        mesh=mesh,
        in_specs=(
            P("stn", "cell", None, None, None),
            P("stn", "cell", None),
            P("cell", None),
            P("cell", None),
            P(("stn", "cell"), None),
            P(("stn", "cell"), None),
        ),
        out_specs=(P(("stn", "cell"), None), P(("stn", "cell"), None)),
        check_vma=False,
    )
```

```python
import jax
import jax.numpy as jnp
from jax import lax
from jax.experimental import pallas as pl
from jax.experimental.pallas import tpu as pltpu
from jax.sharding import PartitionSpec as P

MESH = pl.DeviceIdType.MESH
ITERS = 3
SLOTS, BLOCK, MARGINS, CENTRES, MEMBERS = 2, 512, 4, 32, 128
NX, NZ, NY = 4, 8, 8
NSTN, NCELL = NX * NZ, NY * 2
F32, BF16 = jnp.float32, jnp.bfloat16


def split(value):
    high = value.astype(BF16)
    low = (value - high.astype(F32)).astype(BF16)
    return high, low


def wide(value):
    return jnp.concatenate(split(value), axis=1)


def column_sum(value):
    return jnp.sum(value.reshape(-1, MEMBERS), axis=0, keepdims=True)


def interleave(first, second):
    upper = lax.broadcasted_iota(jnp.int32, first.shape, 1) < MARGINS
    even = jnp.where(upper, first, pltpu.roll(second, MARGINS, 1))
    odd = jnp.where(upper, pltpu.roll(first, MARGINS, 1), second)
    return even, odd


def kernel(
    sens_hbm, blocks_hbm, margin_hbm, centres_hbm, controls, observed_hbm, outputs,
    blocks, margin, centres, observed, sens, sens_t, basis, basis_r, basis_t, coeff_rhs, cell_rhs, slope, pulled,
    list_in, hits, hot, hot_t, same, entry_rhs,
    gath, part, core_in, paired, y_in, full, scat_out, scat_in, ans_out, ans_in,
    own_grad, own_dir, own_image, own_res, own_upd,
    row_core, row_core_in, row_y, row_y_in, row_s, row_s_in, row_c, row_c_in, row_n, row_n_in, row_m, row_m_in, grad_out, grad_in,
    sens_sem, blocks_sem, margin_sem, centres_sem, controls_sem, observed_sem, li_s, li_r, gz_s, gz_r, gx_s, gx_r, hx_s, hx_r, hz_s, hz_r, cc_s, cc_r,
    c_s, c_r, y_s, y_r, fy_s, fy_r, fc_s, fc_r,
    sc_s, sc_r, an_s, an_r, rc_s, rc_r, ry_s, ry_r, rs_s, rs_r, nx_s, nx_r, nz_s, nz_r, gr_s, gr_r,
):
    stn, cell = lax.axis_index("stn"), lax.axis_index("cell")
    x, z = stn // NZ, stn % NZ
    y, core = cell // 2, cell % 2
    def ring(size, step):
        return min(step, size - step)

    far_y = sorted(range(1, NY), key=lambda d: -ring(NY, d))
    far_z = sorted(range(1, NZ), key=lambda d: -ring(NZ, d))
    far_x = sorted(range(1, NX), key=lambda d: -ring(NX, d))
    far_s = sorted(
        [(a, b) for a in range(NX) for b in range(NZ) if a or b],
        key=lambda d: -ring(NX, d[0]) - ring(NZ, d[1]),
    )
    x_peers = [((x + d) % NX, ((x + d) % NX) * NZ + z, cell) for d in far_x]
    z_peers = [((z + d) % NZ, x * NZ + (z + d) % NZ, cell) for d in far_z]
    y_peers = [((y + d) % NY, stn, ((y + d) % NY) * 2 + core) for d in far_y]
    y_others = [((y + d) % NY, stn, ((y + d) % NY) * 2 + 1 - core) for d in far_y]
    core_peer = (1 - core, stn, y * 2 + 1 - core)
    s_peers = [((x + a) % NX * NZ + (z + b) % NZ, (x + a) % NX * NZ + (z + b) % NZ, cell) for a, b in far_s]

    def send(src, dst, ssem, rsem, peer):
        pltpu.make_async_remote_copy(
            src_ref=src, dst_ref=dst, send_sem=ssem, recv_sem=rsem,
            device_id={"stn": peer[1], "cell": peer[2]}, device_id_type=MESH,
        ).start()

    def drain(ref, sem):
        pltpu.make_async_copy(ref, ref, sem).wait()

    barrier = pltpu.get_barrier_semaphore()
    everyone = z_peers + y_peers + x_peers + [core_peer]
    for peer in everyone:
        pl.semaphore_signal(
            barrier, inc=1, device_id={"stn": peer[1], "cell": peer[2]}, device_id_type=MESH
        )
    first = pltpu.make_async_copy(controls, gath.at[x, z], controls_sem)
    first.start()
    small = [
        pltpu.make_async_copy(src, dst, sem) for src, dst, sem in (
            (blocks_hbm, blocks, blocks_sem), (margin_hbm, margin, margin_sem),
            (centres_hbm, centres, centres_sem), (observed_hbm, observed, observed_sem),
        )
    ]
    for copy in small:
        copy.start()
    for half, side in ((0, 1 - core), (1, core)):
        for n in range(SLOTS):
            for p, d in enumerate(far_y + [0]):
                pltpu.make_async_copy(
                    sens_hbm.at[n, (y + d) % NY, side], sens.at[half, n, p], sens_sem.at[half * SLOTS + n]
                ).start()
    first.wait()
    pl.semaphore_wait(barrier, len(everyone))

    most, rest = pl.ds(0, 24), pl.ds(24, 8)
    for peer in z_peers:
        send(gath.at[x, z, most], gath.at[x, z, most], gz_s, gz_r, peer)
    for peer in x_peers:
        send(gath.at[x, z, rest], gath.at[x, z, rest], hx_s, hx_r, peer)

    for copy in small:
        copy.wait()
    listed = [[margin[o, blocks[0, n]] for o in range(MARGINS)] for n in range(SLOTS)]
    entry = lax.broadcasted_iota(jnp.int32, (1, MEMBERS), 1)
    lists = jnp.zeros((1, MEMBERS), F32)
    for n in range(SLOTS):
        for o in range(MARGINS):
            lists = jnp.where(entry == n * MARGINS + o, listed[n][o].astype(F32), lists)
    list_in[stn] = lists
    grad_out[...] = jnp.zeros_like(grad_out)

    lane = lax.broadcasted_iota(jnp.int32, (8, MEMBERS), 1)
    rows_of_centres = [
        jnp.broadcast_to(centres[0:1, i * MEMBERS:(i + 1) * MEMBERS], (8, MEMBERS)) for i in range(8)
    ]
    to_row = lax.broadcasted_iota(jnp.int32, (MEMBERS, MEMBERS), 0)
    to_col = lax.broadcasted_iota(jnp.int32, (MEMBERS, MEMBERS), 1)
    by_row = (to_row == (to_col % MARGINS) * CENTRES + to_col // MARGINS).astype(BF16)
    for n in range(SLOTS):
        block = blocks[0, n]
        centre = jnp.zeros((8, MEMBERS), jnp.int32)
        for o in range(MARGINS):
            j = listed[n][o]
            row = rows_of_centres[0]
            for i in range(1, 8):
                row = jnp.where(j // 4 == i, rows_of_centres[i], row)
            turned = row
            for i in range(1, 4):
                turned = jnp.where((o + 4 - j % 4) % 4 == i, pltpu.roll(row, i * CENTRES, 1), turned)
            centre = jnp.where(lane // CENTRES == o, turned, centre)
        centre = centre[0:1]
        cells = lax.broadcasted_iota(jnp.int32, (BLOCK, MEMBERS), 0) + block * BLOCK
        squared = jnp.zeros((BLOCK, MEMBERS), F32)
        for shift, mask in ((10, 1048575), (5, 31), (0, 31)):
            cell_coord = ((cells >> shift) & mask).astype(F32)
            centre_coord = ((centre >> shift) & mask).astype(F32)
            spread = cell_coord - centre_coord
            squared = squared + spread * spread
        table = jnp.exp(squared * (-0.5 / 100.0))
        high, low = split(table)
        basis[n, :, 0:MEMBERS] = high
        basis[n, :, MEMBERS:] = low
        high = jnp.dot(high, by_row, preferred_element_type=F32)
        low = jnp.dot(low, by_row, preferred_element_type=F32)
        basis_r[n, :, 0:MEMBERS] = high.astype(BF16)
        basis_r[n, :, MEMBERS:] = low.astype(BF16)
        basis_t[n, 0:MEMBERS] = high.T.astype(BF16)
        basis_t[n, MEMBERS:] = low.T.astype(BF16)

    drain(gath.at[0, 0:NZ - 1, most], gz_r)
    for peer in x_peers:
        send(gath.at[x, :, most], gath.at[x, :, most], gx_s, gx_r, peer)
    drain(gath.at[0:NX - 1, 0, rest], hx_r)
    for peer in z_peers:
        send(gath.at[:, z, rest], gath.at[:, z, rest], hz_s, hz_r, peer)
    for half in range(2):
        for n in range(SLOTS):
            drain(sens.at[half, n], sens_sem.at[half * SLOTS + n])
            for i in range(2):
                piece = sens[half, n, i * 4:(i + 1) * 4].reshape(128, BLOCK)
                sens_t[half, n * BLOCK:(n + 1) * BLOCK, i * 128:(i + 1) * 128] = piece.T
    drain(gath.at[0:NX - 1, :, most], gx_r)
    drain(gath.at[:, 0:NZ - 1, rest], hz_r)

    def send_lists():
        for peer in s_peers:
            send(list_in.at[stn], list_in.at[stn], li_s, li_r, peer)

    def use_lists():
        drain(list_in.at[0:NSTN - 1], li_r)
        everyones = jnp.concatenate([list_in[i] for i in range(NSTN)], axis=0)
        number = lax.broadcasted_iota(jnp.int32, (NSTN, MEMBERS), 1).astype(F32)
        for e in range(SLOTS * MARGINS):
            hits[:, e, :] = (everyones[:, e:e + 1] == number).astype(F32)
        found = hits[...].reshape(NSTN * SLOTS * MARGINS, MEMBERS)
        hot[...] = found.astype(BF16)
        found_t = found.T.astype(BF16)
        hot_t[...] = found_t[0:NSTN]
        same[...] = jnp.dot(hot[...], found_t, preferred_element_type=F32).astype(BF16)

    def times_basis(table, n):
        both = jnp.dot(table[n], coeff_rhs[n], preferred_element_type=F32)
        return both[:, 0:MEMBERS] + both[:, MEMBERS:]

    def put_coeffs(n, at, rows, value):
        high, low = split(value)
        for base in (0, MEMBERS):
            coeff_rhs[n, base + at:base + at + rows, 0:MEMBERS] = high
            coeff_rhs[n, base + at:base + at + rows, MEMBERS:] = low

    def both_ways(left, rhs):
        both = jnp.dot(left, rhs, preferred_element_type=F32)
        return both[:, 0:MEMBERS] + both[:, MEMBERS:]

    def station_rows(half, at=slice(0, NY)):
        count = (at.stop - at.start) * CENTRES
        both = jnp.dot(sens[half, 0, at].reshape(count, BLOCK), cell_rhs[0], preferred_element_type=F32)
        both += jnp.dot(sens[half, 1, at].reshape(count, BLOCK), cell_rhs[1], preferred_element_type=F32)
        return (both[:, 0:MEMBERS] + both[:, MEMBERS:]).reshape(-1, CENTRES, MEMBERS)

    def put_cells(n, value):
        high, low = split(value)
        cell_rhs[n, :, 0:MEMBERS] = high
        cell_rhs[n, :, MEMBERS:] = low

    def share_row(i):
        drain(row_core_in.at[i], rc_r.at[i])
        row_y[i] = row_core[i] + row_core_in[i]
        for peer in y_peers:
            send(row_y.at[i], row_y_in.at[i, y], ry_s.at[i], ry_r.at[i], peer)
        row_y_in[i, y] = row_y[i]

    def shared_row(i):
        drain(row_y_in.at[i, 0:NY - 1], ry_r.at[i])
        return sum(row_y_in[i, j] for j in range(NY))

    groups = (slice(0, 3), slice(3, NY))
    place = {d: p for p, d in enumerate(far_y + [0])}

    def sum_cells(k, group_norm=None, meanwhile=None):
        for g, blocks_of in enumerate(groups):
            part[k, blocks_of] = station_rows(0, blocks_of)
            send(part.at[k, blocks_of], core_in.at[k, blocks_of], c_s.at[2 * k + g], c_r.at[2 * k + g], core_peer)
        own_rows = station_rows(1)
        for g, blocks_of in enumerate(groups):
            drain(core_in.at[k, blocks_of], c_r.at[2 * k + g])
            paired[k, blocks_of] = own_rows[blocks_of] + core_in[k, blocks_of]
            for p, peer in list(enumerate(y_peers))[blocks_of]:
                send(paired.at[k, p], y_in.at[k, y], y_s.at[k], y_r.at[k], peer)
            if g == 0 and group_norm is not None:
                row_core[k] = group_norm()
                send(row_core.at[k], row_core_in.at[k], rc_s.at[k], rc_r.at[k], core_peer)
        y_in[k, y] = paired[k, NY - 1]
        if meanwhile is not None:
            meanwhile()
        norm = None
        if group_norm is not None:
            share_row(k)
            norm = shared_row(k)
        drain(y_in.at[k, 0:NY - 1], y_r.at[k])
        return sum(y_in[k, i] for i in range(NY)), norm

    def gather_cells(k, rows, with_curvature=True):
        full[k, 1, NY - 1] = rows
        for p, peer in enumerate(y_peers):
            g = int(p >= 3)
            send(
                full.at[k, 1, NY - 1], full.at[k, 1, place[NY - far_y[p]]],
                fy_s.at[2 * k + g], fy_r.at[2 * k + g], peer,
            )
        if with_curvature:
            row_s[k] = column_sum(rows * rows)
            for peer in s_peers:
                send(row_s.at[k], row_s_in.at[k, stn], rs_s.at[k], rs_r.at[k], peer)
            row_s_in[k, stn] = row_s[k]

    def pull(half, rows):
        return both_ways(sens_t[half], wide(rows)).reshape(SLOTS, BLOCK, MEMBERS)

    def adjoint(k, with_curvature):
        for g, arrived in ((1, slice(3, NY - 1)), (0, slice(0, 3))):
            drain(full.at[k, 1, arrived], fy_r.at[2 * k + g])
            send(
                full.at[k, 1, groups[g]], full.at[k, 0, groups[g]],
                fc_s.at[2 * k + g], fc_r.at[2 * k + g], core_peer,
            )
        pulled[...] = pull(1, full[k, 1].reshape(BLOCK // 2, MEMBERS))
        if with_curvature:
            drain(row_s_in.at[k, 0:NSTN - 1], rs_r.at[k])
            row_core[ITERS + k] = sum(row_s_in[k, i] for i in range(NSTN))
            send(row_core.at[ITERS + k], row_core_in.at[ITERS + k], rc_s.at[ITERS + k], rc_r.at[ITERS + k], core_peer)
        for g in (1, 0):
            drain(full.at[k, 0, groups[g]], fc_r.at[2 * k + g])
        rest_of = pull(0, full[k, 0].reshape(BLOCK // 2, MEMBERS))
        weighted = [wide(slope[n] * (pulled[n] + rest_of[n])) for n in range(SLOTS)]
        if with_curvature:
            share_row(ITERS + k)
        parts = []
        for n in range(SLOTS):
            two = both_ways(basis_t[n], weighted[n])
            parts.append((two[0:MEMBERS] + two[MEMBERS:]).reshape(CENTRES // 2, 2 * MARGINS, MEMBERS))
        even, odd = interleave(parts[0], parts[1])
        scat_out[k, :, 0] = even
        scat_out[k, :, 1] = odd
        for peer in s_peers:
            send(scat_out.at[k, peer[0] // 2, peer[0] % 2], scat_in.at[k, stn], sc_s.at[k], sc_r.at[k], peer)
        scat_in[k, stn] = scat_out[k, stn // 2, stn % 2]
        curvature = None
        if with_curvature:
            curvature = shared_row(ITERS + k)
        drain(scat_in.at[k, 0:NSTN - 1], sc_r.at[k])
        high, low = split(scat_in[k].reshape(NSTN * SLOTS * MARGINS, MEMBERS))
        entry_rhs[:, 0:MEMBERS] = high
        entry_rhs[:, MEMBERS:] = low
        return curvature

    def own_change():
        return both_ways(hot_t[...], entry_rhs[...])

    def answer(k, step=None):
        change = both_ways(same[...], entry_rhs[...]).reshape(NSTN, SLOTS * MARGINS, MEMBERS)
        ans_out[k] = change if step is None else ans_out[k - 1] - step * change
        for peer in s_peers:
            send(ans_out.at[k, peer[0]], ans_in.at[k, stn], an_s.at[k], an_r.at[k], peer)
        ans_in[k, stn] = ans_out[k, stn]
        own = own_change() if step is None else own_grad[...] - step * own_change()
        own_grad[...] = own
        row_n[k] = column_sum(own * own)
        for peer in x_peers:
            send(row_n.at[k], row_n_in.at[k, x], nx_s.at[k], nx_r.at[k], peer)
        row_n_in[k, x] = row_n[k]
        for j in range(NSTN):
            grad_out[j, k:k + 1] = own[j:j + 1]
        drain(row_n_in.at[k, 0:NX - 1], nx_r.at[k])
        row_m[k] = sum(row_n_in[k, i] for i in range(NX))
        for peer in z_peers:
            send(row_m.at[k], row_m_in.at[k, z], nz_s.at[k], nz_r.at[k], peer)
        row_m_in[k, z] = row_m[k]
        if k == ITERS - 1:
            for peer in s_peers:
                send(grad_out.at[peer[0]], grad_in.at[stn], gr_s, gr_r, peer)
            grad_in[stn] = grad_out[stn]

    for n in range(SLOTS):
        for o in range(MARGINS):
            put_coeffs(n, o * CENTRES, CENTRES, gath[listed[n][o] // NZ, listed[n][o] % NZ])
        tanh_phi = jnp.tanh(times_basis(basis, n))
        slope[n] = 0.5 * (1.0 - tanh_phi * tanh_phi)
        put_cells(n, 0.5 * (1.0 + tanh_phi))
    predicted, _ = sum_cells(0, meanwhile=send_lists)
    own_res[...] = observed[...] - predicted
    gather_cells(0, own_res[...], False)
    use_lists()
    adjoint(0, False)
    answer(0)

    norm, ratios, steps = None, [], []
    for k in range(1, ITERS + 1):
        drain(ans_in.at[k - 1, 0:NSTN - 1], an_r.at[k - 1])
        tiles = ans_in[k - 1].reshape(CENTRES // 2, 2, SLOTS * MARGINS, MEMBERS)
        for n, tile in enumerate(interleave(tiles[:, 0], tiles[:, 1])):
            put_coeffs(n, 0, MEMBERS, tile.reshape(MEMBERS, MEMBERS))
        fields = [times_basis(basis_r, n) for n in range(SLOTS)]
        for n in range(SLOTS):
            put_cells(n, slope[n] * fields[n])

        def group_norm():
            drain(row_m_in.at[k - 1, 0:NZ - 1], nz_r.at[k - 1])
            return sum(row_m_in[k - 1, i] for i in range(NZ))

        image, new_norm = sum_cells(k, group_norm)
        ratio = new_norm / norm if k > 1 else None
        if k > 1:
            image = image + ratio * own_image[...]
        norm = new_norm
        own_image[...] = image
        if k < ITERS:
            gather_cells(k, image)
        else:
            row_c[...] = column_sum(image * image)
            for peer in y_others + y_peers + [core_peer]:
                send(row_c, row_c_in.at[cell], cc_s, cc_r, peer)
        ratios.append(ratio)
        if k < ITERS:
            curvature = adjoint(k, True)
            step = norm / curvature
            answer(k, step)
        else:
            row_c_in[cell] = row_c[...]
            drain(grad_in.at[0:NSTN - 1], gr_r)
            for i in range(ITERS):
                direction = jnp.concatenate([grad_in[t, i:i + 1] for t in range(NSTN)], axis=0)
                if i > 0:
                    direction = direction + ratios[i] * own_dir[...]
                own_dir[...] = direction
                if i < ITERS - 1:
                    own_upd[...] = steps[i] * direction if i == 0 else own_upd[...] + steps[i] * direction
            drain(row_c_in.at[0:NCELL - 1], cc_r)
            row_s[0] = sum(row_c_in[i] for i in range(NCELL))
            for peer in s_peers:
                send(row_s.at[0], row_s_in.at[0, stn], rs_s.at[0], rs_r.at[0], peer)
            row_s_in[0, stn] = row_s[0]
            drain(row_s_in.at[0, 0:NSTN - 1], rs_r.at[0])
            step = norm / sum(row_s_in[0, i] for i in range(NSTN))
        own_res[...] = own_res[...] - step * image
        steps.append(step)

    outputs[0:CENTRES] = gath[x, z] + (own_upd[...] + steps[-1] * own_dir[...])
    outputs[CENTRES:] = own_res[...]

    drain(gath.at[0, 0:NZ - 1, most], gz_s)
    drain(gath.at[0:NX - 1, :, most], gx_s)
    drain(gath.at[0:NX - 1, 0, rest], hx_s)
    drain(gath.at[:, 0:NZ - 1, rest], hz_s)
    drain(row_c_in.at[0:NCELL - 1], cc_s)
    drain(grad_in.at[0:NSTN - 1], gr_s)
    drain(list_in.at[0:NSTN - 1], li_s)
    for k in range(ITERS + 1):
        for g in range(2):
            drain(core_in.at[k, groups[g]], c_s.at[2 * k + g])
        drain(y_in.at[k, 0:NY - 1], y_s.at[k])
    for k in range(1, 2 * ITERS):
        drain(row_core_in.at[k], rc_s.at[k])
        drain(row_y_in.at[k, 0:NY - 1], ry_s.at[k])
    for k in range(ITERS):
        for g, arrived in ((1, slice(3, NY - 1)), (0, slice(0, 3))):
            drain(full.at[k, 1, arrived], fy_s.at[2 * k + g])
            drain(full.at[k, 0, groups[g]], fc_s.at[2 * k + g])
        drain(scat_in.at[k, 0:NSTN - 1], sc_s.at[k])
        drain(ans_in.at[k, 0:NSTN - 1], an_s.at[k])
        drain(row_s_in.at[k, 0:NSTN - 1], rs_s.at[k])
        drain(row_n_in.at[k, 0:NX - 1], nx_s.at[k])
        drain(row_m_in.at[k, 0:NZ - 1], nz_s.at[k])


def local(sensitivity, block_list, margin, centres, controls, observed):
    rows = (CENTRES, MEMBERS)
    a, d, r = ITERS + 1, ITERS, 2 * ITERS

    def vmem(*shape):
        return pltpu.VMEM(shape, F32)

    entries = SLOTS * MARGINS
    scratch = [
        pltpu.SMEM((1, SLOTS), jnp.int32),
        pltpu.SMEM((MARGINS, margin.shape[0]), jnp.int32),
        pltpu.VMEM(centres.shape, jnp.int32),
        vmem(*rows),
        pltpu.VMEM((2, SLOTS, NY, CENTRES, BLOCK), BF16),
        pltpu.VMEM((2, SLOTS * BLOCK, BLOCK // 2), BF16),
        pltpu.VMEM((SLOTS, BLOCK, 2 * MEMBERS), BF16),
        pltpu.VMEM((SLOTS, BLOCK, 2 * MEMBERS), BF16),
        pltpu.VMEM((SLOTS, 2 * MEMBERS, BLOCK), BF16),
        pltpu.VMEM((SLOTS, 2 * MEMBERS, 2 * MEMBERS), BF16),
        pltpu.VMEM((SLOTS, BLOCK, 2 * MEMBERS), BF16),
        vmem(SLOTS, BLOCK, MEMBERS),
        vmem(SLOTS, BLOCK, MEMBERS),
        vmem(NSTN, 1, MEMBERS),
        vmem(NSTN, entries, MEMBERS),
        pltpu.VMEM((NSTN * entries, MEMBERS), BF16),
        pltpu.VMEM((NSTN, NSTN * entries), BF16),
        pltpu.VMEM((NSTN * entries, NSTN * entries), BF16),
        pltpu.VMEM((NSTN * entries, 2 * MEMBERS), BF16),
        vmem(NX, NZ, *rows),
        vmem(a, NY, *rows),
        vmem(a, NY, *rows),
        vmem(a, NY, *rows),
        vmem(a, NY, *rows),
        vmem(d, 2, NY, *rows),
        vmem(d, CENTRES // 2, 2, entries, MEMBERS),
        vmem(d, NSTN, entries, MEMBERS),
        vmem(d, NSTN, entries, MEMBERS),
        vmem(d, NSTN, entries, MEMBERS),
        vmem(*rows), vmem(*rows), vmem(*rows), vmem(*rows), vmem(*rows),
        vmem(r, 1, MEMBERS), vmem(r, 1, MEMBERS),
        vmem(r, 1, MEMBERS), vmem(r, NY, 1, MEMBERS),
        vmem(d, 1, MEMBERS), vmem(d, NSTN, 1, MEMBERS),
        vmem(1, MEMBERS), vmem(NCELL, 1, MEMBERS),
        vmem(d, 1, MEMBERS), vmem(d, NX, 1, MEMBERS),
        vmem(d, 1, MEMBERS), vmem(d, NZ, 1, MEMBERS),
        vmem(NSTN, d + 1, MEMBERS), vmem(NSTN, d + 1, MEMBERS),
    ]
    scratch += [pltpu.SemaphoreType.DMA((2 * SLOTS,))]
    scratch += [pltpu.SemaphoreType.DMA] * 17
    scratch += [pltpu.SemaphoreType.DMA((2 * a,))] * 2
    scratch += [pltpu.SemaphoreType.DMA((a,))] * 2
    scratch += [pltpu.SemaphoreType.DMA((2 * d,))] * 4
    scratch += [pltpu.SemaphoreType.DMA((d,))] * 4
    scratch += [pltpu.SemaphoreType.DMA((r,))] * 4
    scratch += [pltpu.SemaphoreType.DMA((d,))] * 6
    scratch += [pltpu.SemaphoreType.DMA] * 2
    in_vmem = pl.BlockSpec(memory_space=pltpu.VMEM)
    outputs = pl.pallas_call(
        kernel,
        out_shape=jax.ShapeDtypeStruct((2 * CENTRES, MEMBERS), F32),
        in_specs=[pl.BlockSpec(memory_space=pl.ANY)] * 6,
        out_specs=in_vmem,
        scratch_shapes=scratch,
        compiler_params=pltpu.CompilerParams(
            collective_id=0, has_side_effects=True, vmem_limit_bytes=60 * 1024 * 1024
        ),
        cost_estimate=pl.CostEstimate(flops=3_000_000_000, bytes_accessed=2_000_000, transcendentals=262144),
        name="gauss_newton",
    )(
        sensitivity.reshape(SLOTS, NY, 2, CENTRES, BLOCK), block_list.reshape(1, SLOTS), margin.T, centres,
        controls, observed,
    )
    return outputs[:CENTRES], outputs[CENTRES:]


def solution(mesh):
    return jax.shard_map(
        local,
        mesh=mesh,
        in_specs=(
            P("stn", "cell", None, None, None),
            P("stn", "cell", None),
            P("cell", None),
            P("cell", None),
            P(("stn", "cell"), None),
            P(("stn", "cell"), None),
        ),
        out_specs=(P(("stn", "cell"), None), P(("stn", "cell"), None)),
        check_vma=False,
    )
```
